512 devices in a mesh: ctx: 64 (over x, y, z_lo), exp: 8 (over z_hi, core).
Axes of the slice: x: 4, y: 8, z: 8 (z_hi: 4, z_lo: 2; z = z_hi * 2 + z_lo), core: 2. Of those that a mesh axis runs over, the one named last changes fastest.
Arguments:
- queries: bfloat16 [8192, 4096], P('ctx', 'exp'), may hold values from -14 to 14
- key_rows: bfloat16 [8192, 256], P('ctx'), may hold values from -14 to 14
- value_rows: bfloat16 [8192, 256], P('ctx'), may hold values from -6 to 6
- out_weight: bfloat16 [4096, 4096], P('ctx', 'exp'), may hold values from -0.09375 to 0.09375
- residual: bfloat16 [8192, 4096], P('ctx', 'exp'), may hold values from -6 to 6
- norm_gain: float32 [4096], P('exp'), may hold values from 0.25 to 1.75
- w_gate: bfloat16 [64, 4096, 768], P('ctx', 'exp'), may hold values from -0.09375 to 0.09375
- w_up: bfloat16 [64, 4096, 768], P('ctx', 'exp'), may hold values from -0.09375 to 0.09375
- w_down: bfloat16 [64, 768, 4096], P('ctx', None, 'exp'), may hold values from -0.21875 to 0.21875
- pred_ids: int32 [8192, 8], P('ctx'), may hold values from 0 to 63, all different within a row; in each aligned block of 128 rows (0 to 127, 128 to 255, ...) at most 19 rows name the same one
- route_gates: bfloat16 [8192, 8], P('ctx'), may hold values from 0.049804688 to 0.29882812
- fix_pair: int32 [64, 32], P('ctx'), may hold values from 0 to 1023, as said below
- fix_expert: int32 [64, 32], P('ctx'), may hold values from 0 to 63, as said below
- fix_count: int32 [64], P('ctx'), may hold values from 2 to 32
Outputs:
- stream_out: bfloat16 [8192, 4096], P('ctx', 'exp')
- expert_out: bfloat16 [8192, 4096], P('ctx', 'exp')
The draws below stay inside these ranges and needn't reach their ends.
Inputs may be any that keep to these rules, and one draw needn't show every extreme that they name: `pred_ids`: within the rows of one device (128 tokens), no expert is named more than 19 times; the 8 ids of a token differ. `fix_pair`: A device's entries are distinct choices of its own tokens; only its first fix_count entries are listed. `fix_expert`: among one device's listed entries no expert appears more than 2 times; the first 2 entries of every device name one common expert.
All inputs are finite; a program needn't handle non-finite values.
Results may differ from the reference program's by a relative error of at most 0.029.
Values may be sent and summed in bfloat16 or wider, within the bound.
No kernel may reach another device: no remote copies, remote signals or barrier semaphores. Data moves between devices by JAX's collectives and lax.ppermute only.
A program may use at most 64 MiB of HBM per device.

```python
import math
import jax
import jax.numpy as jnp
import numpy as np
from jax import lax

D = 4096
HD = 128
TOPK = 8
QH = 32
KVH = 2
FF = 768
FIX = 32
FCAP = 2
TOK = 128
TOKENS = 8192
EXPERTS = 64
CAP = 19
N_CTX = 64
N_EXP = 8


def draw_queries(key, part):
    key = jax.random.fold_in(key, 1)
    drawn = jnp.clip(jax.random.normal(key, (TOKENS, QH * HD), jnp.float32), -6.0, 6.0)
    return drawn.astype(jnp.bfloat16)


def draw_key_rows(key, part):
    key = jax.random.fold_in(key, 2)
    drawn = jnp.clip(jax.random.normal(key, (TOKENS, KVH * HD), jnp.float32), -6.0, 6.0)
    return drawn.astype(jnp.bfloat16)


def draw_fix_pair(key, part):
    key = jax.random.fold_in(key, 3)
    row_keys = jax.random.split(key, N_CTX)

    def one_row(row_key):
        return jax.random.permutation(row_key, TOK * TOPK)[:FIX]
    return jax.vmap(one_row)(row_keys).astype(jnp.int32)


def draw_fix_expert(key, part):
    key = jax.random.fold_in(key, 5)
    common = jax.random.randint(jax.random.fold_in(key, 1), (), 0, EXPERTS)
    row_keys = jax.random.split(jax.random.fold_in(key, 2), N_CTX)

    def one_row(row_key):
        others = jax.random.permutation(row_key, EXPERTS - 1)
        position = jnp.arange(FIX)
        spread = others[jnp.maximum(position - FCAP, 0) % (EXPERTS - 1)]
        return jnp.where(position < FCAP, common, (common + 1 + spread) % EXPERTS)
    return jax.vmap(one_row)(row_keys).astype(jnp.int32)


def draw_fix_count(key, part):
    key = jax.random.fold_in(key, 7)
    counts = jax.random.randint(jax.random.fold_in(key, 1), (N_CTX,), FCAP, FIX + 1)
    fullest = jax.random.randint(jax.random.fold_in(key, 2), (), 0, N_CTX)
    return jnp.where(jnp.arange(N_CTX) == fullest, FIX, counts).astype(jnp.int32)


def level_of(stream_key, extent, cuts, smallest, largest):
    loudness, own = 1.0, jax.random.fold_in(stream_key, 6)
    for axis_at, parts in cuts:
        heights = jnp.exp(jax.random.uniform(jax.random.fold_in(own, axis_at), (parts,), jnp.float32, smallest / len(cuts), largest / len(cuts)))
        loudness = loudness * jnp.repeat(heights, extent[axis_at] // parts).reshape([-1 if axis == axis_at else 1 for axis in range(len(extent))])
    return loudness


def deal_out(key, own, number, rows, amount, top, most, slope):
    sequence = jax.random.permutation(key, amount)
    heavy_load, ordinary = shares(amount, rows * top, most, slope, True), shares(amount, rows * top, most, slope, False)
    places = jnp.arange(amount)

    def named(lengths, offset_by):
        used = int((lengths > 0).sum())
        fixed = max(1, used // 4)
        shifted = fixed + (places - fixed + offset_by * (used - fixed)) % max(1, amount - fixed)
        return jnp.zeros((amount,), jnp.int32).at[sequence[jnp.where(places < fixed, places, shifted)]].set(jnp.asarray(lengths, jnp.int32))

    lengths = jnp.where(number % 4 == 0, named(heavy_load, number // 4), named(ordinary, number - number // 4 - 1))
    mixed = jax.random.permutation(jax.random.fold_in(own, 3), amount)
    source_of, receiver = mixed[0:amount // 2 * 2:2], mixed[1:amount // 2 * 2:2]
    slack = jnp.minimum(lengths[source_of] - 1, most - lengths[receiver]) // 2
    slack = jnp.where((source_of == sequence[0]) | (receiver == sequence[0]) | (lengths[receiver] == 0), 0, jnp.maximum(slack, 0))
    shifted = jax.random.randint(jax.random.fold_in(own, 4), (amount // 2,), 0, 1 << 20) % (slack + 1)
    lengths = lengths.at[source_of].add(-shifted).at[receiver].add(shifted)
    labels = jnp.searchsorted(jnp.cumsum(lengths), jnp.arange(rows * top), side="right").astype(jnp.int32)
    listing = labels.reshape(top, rows).T
    listing = listing[jax.random.permutation(jax.random.fold_in(own, 1), rows)]
    offset_by = jax.random.randint(jax.random.fold_in(own, 2), (rows, 1), 0, top)
    return jnp.take_along_axis(listing, (jnp.arange(top)[None, :] + offset_by) % top, axis=1)


def shares(count, total, reach, skew, full):
    portions = [(1 << 20) // math.isqrt(grade ** skew) + 1 for grade in range(1, count + 1)]
    largest = reach if full else min(reach, max(-(-total // count), total * portions[0] // sum(portions)))
    least = 1 if total - largest >= count - 1 else 0
    holding, surplus = [largest] + [least] * (count - 1), total - largest - least * (count - 1)
    while surplus > 0:
        candidates = [i for i in range(1, count) if holding[i] < largest] or [i for i in range(1, count) if holding[i] < reach]
        pool, budget = sum([portions[i] for i in candidates]), surplus
        for i in candidates:
            addition = min(reach - holding[i], max(1, budget * portions[i] // pool), surplus)
            holding[i] = holding[i] + addition
            surplus = surplus - addition
    return np.array(holding)


def bell_draw(rng, extent, deviation, limit, cuts=(), kind=jnp.bfloat16):
    drawn = deviation * jax.random.normal(rng, extent, jnp.float32)
    if cuts:
        drawn = drawn * level_of(rng, extent, cuts, -0.22, 0.18)
    return jnp.clip(drawn, -limit, limit).astype(kind)


def setup_inputs(seed: int = 0) -> dict:
    seeds = jax.random.split(jax.random.key(seed), 15)
    queries = draw_queries(jax.random.fold_in(seeds[14], 71), 0)
    key_rows = draw_key_rows(jax.random.fold_in(seeds[14], 71), 0)
    value_rows = bell_draw(seeds[2], (TOKENS, KVH * HD), 1.0, 6.0, ((0, 64),))
    out_weight = bell_draw(seeds[3], (QH * HD, D), (QH * HD) ** -0.5, 0.09375, ((0, 64), (1, 8)))
    residual = bell_draw(seeds[4], (TOKENS, D), 1.0, 6.0, ((0, 64), (1, 8)))
    norm_gain = jnp.clip(1.0 + 0.15 * jax.random.normal(seeds[5], (D,), jnp.float32), 0.25, 1.75)
    w_gate = bell_draw(seeds[6], (EXPERTS, D, FF), D ** -0.5, 0.09375, ((0, 64), (1, 8)))
    w_up = bell_draw(seeds[7], (EXPERTS, D, FF), D ** -0.5, 0.09375, ((0, 64), (1, 8)))
    w_down = bell_draw(seeds[8], (EXPERTS, FF, D), FF ** -0.5, 0.21875, ((0, 64), (2, 8)))
    pred_ids_keys = jax.random.split(jax.random.fold_in(seeds[9], 1), TOKENS // TOK)
    pred_ids_turns = jax.random.permutation(jax.random.fold_in(seeds[9], 3), TOKENS // TOK)
    pred_ids = jax.vmap(lambda own, number: deal_out(jax.random.fold_in(seeds[9], 2), own, number, TOK, EXPERTS, TOPK, CAP, 1))(pred_ids_keys, pred_ids_turns).reshape((TOKENS, TOPK))
    route_gates = jnp.clip(0.049804688 + 0.24902344 * jax.random.uniform(seeds[10], (TOKENS, TOPK), jnp.float32) ** level_of(seeds[10], (TOKENS, TOPK), ((0, 64),), -0.2, 0.2), 0.049804688, 0.29882812).astype(jnp.bfloat16)
    fix_pair = draw_fix_pair(jax.random.fold_in(seeds[14], 71), 0)
    fix_expert = draw_fix_expert(jax.random.fold_in(seeds[14], 71), 0)
    fix_count = draw_fix_count(jax.random.fold_in(seeds[14], 71), 0)
    return dict(queries=queries, key_rows=key_rows, value_rows=value_rows, out_weight=out_weight, residual=residual, norm_gain=norm_gain, w_gate=w_gate, w_up=w_up, w_down=w_down, pred_ids=pred_ids, route_gates=route_gates, fix_pair=fix_pair, fix_expert=fix_expert, fix_count=fix_count)


epsilon = 1e-06

def rounded(values):
    return lax.optimization_barrier(values.astype(jnp.bfloat16)).astype(jnp.float32)

def window_attention(queries, key_rows, value_rows):
    group_size = QH // KVH
    score_scale = 1.0 / HD ** 0.5
    padding = jnp.zeros((3 * TOK, KVH * HD), jnp.bfloat16)
    padded_keys = jnp.concatenate([padding, key_rows], axis=0)
    padded_values = jnp.concatenate([padding, value_rows], axis=0)

    def one_block(block_id):
        first_row = (block_id * TOK).astype(jnp.int32)
        q_view = lax.dynamic_slice_in_dim(queries, first_row, TOK, 0).astype(jnp.float32).reshape(TOK, KVH, group_size, HD)
        k_view = lax.dynamic_slice_in_dim(padded_keys, first_row, 4 * TOK, 0).astype(jnp.float32).reshape(4 * TOK, KVH, HD)
        v_view = lax.dynamic_slice_in_dim(padded_values, first_row, 4 * TOK, 0).astype(jnp.float32).reshape(4 * TOK, KVH, HD)
        scores = jnp.einsum('tkgd,skd->kgts', q_view, k_view) * score_scale
        q_pos = first_row + jnp.arange(TOK, dtype=jnp.int32)
        k_pos = first_row - 3 * TOK + jnp.arange(4 * TOK, dtype=jnp.int32)
        allowed = (k_pos[None, :] >= 0) & (k_pos[None, :] <= q_pos[:, None])
        scores = jnp.where(allowed, scores, -1e+30)
        highest = lax.optimization_barrier(jnp.max(scores, axis=3, keepdims=True))
        weights = jnp.where(allowed, jnp.exp(scores - highest), 0.0)
        denominators = lax.optimization_barrier(jnp.sum(weights, axis=3, keepdims=True))
        mixed_out = jnp.einsum('kgts,skd->kgtd', rounded(weights), v_view) / denominators
        return jnp.transpose(mixed_out, (2, 0, 1, 3)).reshape(TOK, QH * HD).astype(jnp.bfloat16)
    blocks_out = lax.map(one_block, jnp.arange(N_CTX, dtype=jnp.int32))
    return blocks_out.reshape(TOK * N_CTX, QH * HD)

def reference(queries, key_rows, value_rows, out_weight, residual, norm_gain, w_gate, w_up, w_down, pred_ids, route_gates, fix_pair, fix_expert, fix_count):
    attended = window_attention(queries, key_rows, value_rows)
    projected = jnp.dot(attended, out_weight, preferred_element_type=jnp.float32)
    stream = residual.astype(jnp.float32) + projected
    squares = lax.optimization_barrier(jnp.sum(stream * stream, axis=1, keepdims=True))
    normed = (stream * lax.rsqrt(squares / D + epsilon) * norm_gain[None, :]).astype(jnp.bfloat16)
    slot_total = TOKENS * TOPK
    live_fix = jnp.arange(FIX, dtype=jnp.int32)[None, :] < fix_count[:, None]
    offsets = (jnp.arange(N_CTX, dtype=jnp.int32) * (TOK * TOPK))[:, None]
    targets = jnp.where(live_fix, fix_pair + offsets, slot_total).reshape(-1).astype(jnp.int32)
    true_ids = pred_ids.reshape(-1).at[targets].set(fix_expert.reshape(-1), mode='drop')
    gate_flat = route_gates.reshape(-1).astype(jnp.float32)
    row_limit = N_CTX * (CAP + FCAP)
    slice_width = D // N_EXP

    def expert_step(running, inputs):
        gate_matrix, up_matrix, down_matrix, expert_id = inputs
        matches = true_ids == expert_id
        picked = jnp.nonzero(matches, size=row_limit, fill_value=0)[0].astype(jnp.int32)
        present = jnp.arange(row_limit, dtype=jnp.int32) < jnp.sum(matches.astype(jnp.int32))
        token_ids = picked // TOPK
        rows_in = normed[token_ids].astype(jnp.float32).reshape(row_limit, N_EXP, slice_width)
        gate_blocks = gate_matrix.astype(jnp.float32).reshape(N_EXP, slice_width, FF)
        up_blocks = up_matrix.astype(jnp.float32).reshape(N_EXP, slice_width, FF)
        gate_sum = lax.optimization_barrier(jnp.sum(rounded(jnp.einsum('rjd,jdf->rjf', rows_in, gate_blocks)), axis=1))
        up_sum = lax.optimization_barrier(jnp.sum(rounded(jnp.einsum('rjd,jdf->rjf', rows_in, up_blocks)), axis=1))
        hidden = (jax.nn.silu(gate_sum) * up_sum).astype(jnp.bfloat16)
        outputs = rounded(jnp.dot(hidden, down_matrix, preferred_element_type=jnp.float32))
        scales = jnp.where(present, gate_flat[picked], 0.0)
        return (running.at[token_ids].add(scales[:, None] * outputs), None)
    initial = jnp.zeros((TOKENS, D), jnp.float32)
    combined, ignored = lax.scan(expert_step, initial, (w_gate, w_up, w_down, jnp.arange(EXPERTS, dtype=jnp.int32)))
    return (stream.astype(jnp.bfloat16), combined.astype(jnp.bfloat16))
```

```python
import jax
import jax.numpy as jnp
import numpy as np
from jax import lax
from jax.sharding import Mesh, PartitionSpec as P

D = 4096
HD = 128
TOPK = 8
QH = 32
KVH = 2
FF = 768
FIX = 32
TOK = 128
SLOTS = 21
NX, NY, NL, NH, NC = 4, 8, 2, 4, 2
N_CTX = NX * NY * NL
ROWS = N_CTX * SLOTS
SHARE = ROWS // NX
SLICE = D // (NH * NC)
CTX = ("x", "y", "l")
HOME = ("h", "y", "l")
f32, bf16 = jnp.float32, jnp.bfloat16

epsilon = 1e-06


def turn(block):
    route = [(a * NH + b, b * NX + a) for a in range(NX) for b in range(NH)]
    return lax.ppermute(block, ("x", "h"), route)


def swap(block, axis):
    return lax.ppermute(block, axis, [(0, 1), (1, 0)])


def from_behind(block, distance):
    route = [(i, i + distance) for i in range(N_CTX - distance)]
    return lax.ppermute(block, CTX, route)


def attention(queries, key_rows, value_rows):
    tokens = queries.shape[0]
    block = lax.axis_index(CTX)
    kv_first = lax.axis_index("h") // 2 * HD
    own = jnp.concatenate(
        [
            lax.dynamic_slice_in_dim(key_rows, kv_first, HD, 1),
            lax.dynamic_slice_in_dim(value_rows, kv_first, HD, 1),
        ],
        axis=1,
    )
    pairs = [from_behind(own, 3), from_behind(own, 2), from_behind(own, 1), own]
    keys = jnp.concatenate([pair[:, :HD] for pair in pairs], axis=0)
    values = jnp.concatenate([pair[:, HD:] for pair in pairs], axis=0)
    q_view = queries.reshape(tokens, -1, HD)
    scores = jnp.einsum("tgd,sd->gts", q_view, keys, preferred_element_type=f32) / HD**0.5
    q_pos = block * tokens + jnp.arange(tokens)
    k_pos = (block - 3) * tokens + jnp.arange(4 * tokens)
    allowed = (k_pos[None, :] >= 0) & (k_pos[None, :] <= q_pos[:, None])
    scores = jnp.where(allowed, scores, -1e30)
    highest = jnp.max(scores, axis=2, keepdims=True)
    weights = jnp.where(allowed, jnp.exp(scores - highest), 0.0)
    denominators = jnp.sum(weights, axis=2, keepdims=True)
    mixed = (
        jnp.einsum("gts,sd->gtd", weights.astype(bf16), values, preferred_element_type=f32)
        / denominators
    )
    return jnp.transpose(mixed, (1, 0, 2)).reshape(tokens, -1).astype(bf16)


def slots_of(pred_ids, fix_pair, fix_expert, fix_count):
    tokens = pred_ids.shape[0]
    places = jnp.arange(tokens * TOPK, dtype=jnp.int32).reshape(tokens, TOPK)
    live = jnp.arange(FIX) < fix_count[0]
    hit = (places[:, :, None] == fix_pair[0][None, None, :]) & live[None, None, :]
    fixed = jnp.sum(jnp.where(hit, fix_expert[0][None, None, :], 0), axis=2)
    ids = jnp.where(jnp.any(hit, axis=2), fixed, pred_ids)
    named = ids[:, :, None] == jnp.arange(N_CTX)[None, None, :]
    counts = jnp.sum(named.astype(f32), axis=1)
    earlier = (
        jnp.arange(tokens)[:, None] > jnp.arange(tokens)[None, :]
    ).astype(bf16)
    before = jnp.dot(earlier, counts.astype(bf16), preferred_element_type=f32)
    rank = jnp.sum(jnp.where(named, before[:, None, :], 0.0), axis=2)
    twin = (ids[:, :, None] == ids[:, None, :]) & (
        jnp.arange(TOPK)[None, :, None] > jnp.arange(TOPK)[None, None, :]
    )
    rank = rank + jnp.sum(twin.astype(f32), axis=2)
    return ids.astype(f32) * SLOTS + rank


def body(
    queries,
    key_rows,
    value_rows,
    out_weight,
    residual,
    norm_gain,
    w_gate,
    w_up,
    w_down,
    pred_ids,
    route_gates,
    fix_pair,
    fix_expert,
    fix_count,
):
    core = lax.axis_index("c")
    tokens = queries.shape[0]
    half = FF // 2

    strip = turn(out_weight)
    other_strip = swap(strip, "l")
    first = lax.axis_index("l") == 0
    strips = jnp.concatenate(
        [jnp.where(first, strip, other_strip), jnp.where(first, other_strip, strip)], axis=0
    )
    quarter = lax.all_gather(strips, "y", axis=0, tiled=True)

    slots = slots_of(pred_ids, fix_pair, fix_expert, fix_count)
    table = turn(jnp.concatenate([slots, route_gates.astype(f32)], axis=1)).T
    slot_rows, gate_rows = table[:TOPK], table[TOPK:]
    row_ids = jnp.arange(ROWS, dtype=f32)[:, None]
    row_map = jnp.zeros((ROWS, tokens), f32)
    combine = jnp.zeros((ROWS, tokens), f32)
    for k in range(TOPK):
        here = slot_rows[k][None, :] == row_ids
        row_map = row_map + jnp.where(here, 1.0, 0.0)
        combine = combine + jnp.where(here, gate_rows[k][None, :], 0.0)
    row_map, combine = row_map.astype(bf16), combine.astype(bf16)

    def columns(which):
        return jnp.concatenate(
            [
                lax.dynamic_slice_in_dim(w_gate[0], which * half, half, 1),
                lax.dynamic_slice_in_dim(w_up[0], which * half, half, 1),
            ],
            axis=1,
        )

    gate_up = turn(jnp.concatenate([columns(core), swap(columns(1 - core), "c")], axis=0))
    down = turn(w_down[0])
    gain = turn(norm_gain[None, :])
    inverse = 1.0 / (gain * gain)
    other_inverse = swap(inverse, "c")
    residual_here = turn(residual)

    attended = attention(queries, key_rows, value_rows)
    heads = lax.all_gather(attended, "x", axis=0, tiled=True)
    other_heads = swap(heads, "c")
    partial = jnp.dot(
        heads,
        lax.dynamic_slice_in_dim(quarter, core * SLICE, SLICE, 0),
        preferred_element_type=f32,
    ) + jnp.dot(
        other_heads,
        lax.dynamic_slice_in_dim(quarter, (1 - core) * SLICE, SLICE, 0),
        preferred_element_type=f32,
    )
    terms = lax.all_to_all(
        partial.astype(bf16).reshape(NH, tokens, SLICE), "h", split_axis=0, concat_axis=0, tiled=True
    )
    stream = residual_here.astype(f32) + jnp.sum(terms.astype(f32), axis=0)
    stream_out = turn(stream.astype(bf16))

    scaled = (stream * gain).astype(bf16)
    outgoing = jnp.dot(row_map, scaled, preferred_element_type=f32).astype(bf16)
    incoming = lax.all_to_all(
        outgoing.reshape(N_CTX, SLOTS, SLICE), HOME, split_axis=0, concat_axis=0, tiled=True
    ).reshape(ROWS, SLICE)
    other_incoming = swap(incoming, "c")
    gate_up_part = (
        jnp.dot(incoming, gate_up[:SLICE], preferred_element_type=f32)
        + jnp.dot(other_incoming, gate_up[SLICE:], preferred_element_type=f32)
    ).astype(bf16)

    def squares(rows, weight):
        return jnp.sum(jnp.square(rows.astype(f32)) * weight, axis=1)

    square_part = (squares(incoming, inverse) + squares(other_incoming, other_inverse)).reshape(
        NX, 1, SHARE
    )
    high = square_part.astype(bf16)
    low = (square_part - high.astype(f32)).astype(bf16)
    extra = jnp.concatenate([high, low], axis=1)
    extra = jnp.pad(extra, ((0, 0), (0, 14), (0, FF - SHARE)))
    parts = lax.all_to_all(
        jnp.concatenate([gate_up_part.reshape(NX, SHARE, FF), extra], axis=1),
        "x",
        split_axis=0,
        concat_axis=0,
        tiled=True,
    ).astype(f32)
    sums = jnp.sum(parts[:, :SHARE], axis=0)
    total = jnp.sum(parts[:, SHARE : SHARE + 2, :SHARE], axis=(0, 1))
    sums = sums * lax.rsqrt(total / D + epsilon)[:, None]
    hidden = (jax.nn.silu(sums[:, :half]) * sums[:, half:]).astype(bf16)
    all_hidden = lax.all_gather(hidden, "x", axis=0, tiled=True)
    other_hidden = swap(all_hidden, "c")
    results = (
        jnp.dot(
            all_hidden,
            lax.dynamic_slice_in_dim(down, core * half, half, 0),
            preferred_element_type=f32,
        )
        + jnp.dot(
            other_hidden,
            lax.dynamic_slice_in_dim(down, (1 - core) * half, half, 0),
            preferred_element_type=f32,
        )
    ).astype(bf16)
    returned = lax.all_to_all(
        results.reshape(N_CTX, SLOTS, SLICE), HOME, split_axis=0, concat_axis=0, tiled=True
    ).reshape(ROWS, SLICE)
    mixed = jnp.einsum("rt,rd->td", combine, returned, preferred_element_type=f32)
    return stream_out, turn(mixed.astype(bf16))


def solution(mesh):
    split = Mesh(np.asarray(mesh.devices).reshape(NX, NY, NL, NH, NC), ("x", "y", "l", "h", "c"))
    ctx, exp = CTX, ("h", "c")
    placed = (
        P(ctx, exp),
        P(ctx, None),
        P(ctx, None),
        P(ctx, exp),
        P(ctx, exp),
        P(exp),
        P(ctx, exp, None),
        P(ctx, exp, None),
        P(ctx, None, exp),
        P(ctx, None),
        P(ctx, None),
        P(ctx, None),
        P(ctx, None),
        P(ctx),
    )
    return jax.shard_map(
        body,
        mesh=split,
        in_specs=placed,
        out_specs=(P(ctx, exp), P(ctx, exp)),
        check_vma=False,
    )
```

```python
import jax
import jax.numpy as jnp
import numpy as np
from jax import lax
from jax.sharding import Mesh, PartitionSpec as P

D = 4096
HD = 128
TOPK = 8
QH = 32
KVH = 2
FF = 768
FIX = 32
TOK = 128
SLOTS = 21
NX, NY, NL, NH, NC = 4, 8, 2, 4, 2
N_CTX = NX * NY * NL
GRID = NX * NY
ROWS = GRID * SLOTS
SHARE = ROWS // NH
SLICE = D // (NH * NC)
CTX = ("x", "y", "l")
f32, bf16 = jnp.float32, jnp.bfloat16

epsilon = 1e-06


def turn(block):
    route = [(a * NH + b, b * NX + a) for a in range(NX) for b in range(NH)]
    return lax.ppermute(block, ("x", "h"), route)


def swap(block, axis):
    return lax.ppermute(block, axis, [(0, 1), (1, 0)])


def cycle(block):
    return lax.ppermute(block, ("l", "c"), [(0, 3), (3, 2), (2, 1), (1, 0)])


def cycle_back(block):
    return lax.ppermute(block, ("l", "c"), [(3, 0), (2, 3), (1, 2), (0, 1)])


def across(block):
    return lax.ppermute(block, ("l", "c"), [(1, 3), (3, 1)])


def from_behind(block, distance):
    route = [(i, i + distance) for i in range(N_CTX - distance)]
    return lax.ppermute(block, CTX, route)


def attention(queries, key_rows, value_rows):
    tokens = queries.shape[0]
    block = lax.axis_index(CTX)
    kv_first = lax.axis_index("h") // 2 * HD
    own = jnp.concatenate(
        [
            lax.dynamic_slice_in_dim(key_rows, kv_first, HD, 1),
            lax.dynamic_slice_in_dim(value_rows, kv_first, HD, 1),
        ],
        axis=1,
    )
    pairs = [from_behind(own, 3), from_behind(own, 2), from_behind(own, 1), own]
    keys = jnp.concatenate([pair[:, :HD] for pair in pairs], axis=0)
    values = jnp.concatenate([pair[:, HD:] for pair in pairs], axis=0)
    q_view = queries.reshape(tokens, -1, HD)
    scores = jnp.einsum("tgd,sd->gts", q_view, keys, preferred_element_type=f32) / HD**0.5
    q_pos = block * tokens + jnp.arange(tokens)
    k_pos = (block - 3) * tokens + jnp.arange(4 * tokens)
    allowed = (k_pos[None, :] >= 0) & (k_pos[None, :] <= q_pos[:, None])
    scores = jnp.where(allowed, scores, -1e30)
    highest = jnp.max(scores, axis=2, keepdims=True)
    weights = jnp.where(allowed, jnp.exp(scores - highest), 0.0)
    denominators = jnp.sum(weights, axis=2, keepdims=True)
    mixed = (
        jnp.einsum("gts,sd->gtd", weights.astype(bf16), values, preferred_element_type=f32)
        / denominators
    )
    return jnp.transpose(mixed, (1, 0, 2)).reshape(tokens, -1).astype(bf16)


def slots_of(pred_ids, fix_pair, fix_expert, fix_count):
    tokens = pred_ids.shape[0]
    places = jnp.arange(tokens * TOPK, dtype=jnp.int32).reshape(tokens, TOPK)
    live = jnp.arange(FIX) < fix_count[0]
    hit = (places[:, :, None] == fix_pair[0][None, None, :]) & live[None, None, :]
    fixed = jnp.sum(jnp.where(hit, fix_expert[0][None, None, :], 0), axis=2)
    ids = jnp.where(jnp.any(hit, axis=2), fixed, pred_ids)
    named = ids[:, :, None] == jnp.arange(N_CTX)[None, None, :]
    counts = jnp.sum(named.astype(f32), axis=1)
    earlier = (
        jnp.arange(tokens)[:, None] > jnp.arange(tokens)[None, :]
    ).astype(bf16)
    before = jnp.dot(earlier, counts.astype(bf16), preferred_element_type=f32)
    rank = jnp.sum(jnp.where(named, before[:, None, :], 0.0), axis=2)
    twin = (ids[:, :, None] == ids[:, None, :]) & (
        jnp.arange(TOPK)[None, :, None] > jnp.arange(TOPK)[None, None, :]
    )
    rank = rank + jnp.sum(twin.astype(f32), axis=2)
    return ids.astype(f32), rank


def body(
    queries,
    key_rows,
    value_rows,
    out_weight,
    residual,
    norm_gain,
    w_gate,
    w_up,
    w_down,
    pred_ids,
    route_gates,
    fix_pair,
    fix_expert,
    fix_count,
):
    core, side = lax.axis_index("c"), lax.axis_index("l")
    tokens = queries.shape[0]

    other_strip = swap(out_weight, "l")
    strips = jnp.concatenate(
        [
            jnp.where(side == 0, out_weight, other_strip),
            jnp.where(side == 0, other_strip, out_weight),
        ],
        axis=0,
    )
    quarter = lax.all_gather(strips, "y", axis=0, tiled=True)

    ids, rank = slots_of(pred_ids, fix_pair, fix_expert, fix_count)
    table = jnp.concatenate([ids, rank, route_gates.astype(f32)], axis=1)
    table = jnp.where(core == 0, table, swap(table, "l")).T
    ids, rank, gates = table[:TOPK], table[TOPK : 2 * TOPK], table[2 * TOPK :]
    column = jnp.floor(ids * 0.5)
    slots = jnp.where(ids - 2.0 * column == side.astype(f32), column * SLOTS + rank, -1.0)
    row_ids = jnp.arange(ROWS, dtype=f32)[:, None]
    row_map = jnp.zeros((ROWS, tokens), f32)
    combine = jnp.zeros((ROWS, tokens), f32)
    for k in range(TOPK):
        here = slots[k][None, :] == row_ids
        row_map = row_map + jnp.where(here, 1.0, 0.0)
        combine = combine + jnp.where(here, gates[k][None, :], 0.0)
    row_map, combine = row_map.astype(bf16), combine.astype(bf16)

    gate_up = jnp.concatenate([w_gate[0], w_up[0]], axis=1)
    other_gate_up = swap(gate_up, "c")
    down = jnp.concatenate([w_down[0], swap(w_down[0], "c")], axis=1)
    gain = norm_gain[None, :]
    inverse = 1.0 / (gain * gain)
    other_inverse = swap(inverse, "c")

    attended = turn(attention(queries, key_rows, value_rows))
    heads = lax.all_gather(attended, "h", axis=0, tiled=True)
    other_heads = swap(heads, "c")
    partial = jnp.dot(
        heads,
        lax.dynamic_slice_in_dim(quarter, core * SLICE, SLICE, 0),
        preferred_element_type=f32,
    ) + jnp.dot(
        other_heads,
        lax.dynamic_slice_in_dim(quarter, (1 - core) * SLICE, SLICE, 0),
        preferred_element_type=f32,
    )
    terms = lax.all_to_all(
        partial.astype(bf16).reshape(NX, tokens, SLICE), "x", split_axis=0, concat_axis=0, tiled=True
    )
    stream = residual.astype(f32) + jnp.sum(terms.astype(f32), axis=0)

    scaled = (stream * gain).astype(bf16)
    near, far = cycle(scaled), across(scaled)
    both = jnp.concatenate([jnp.where(core == 0, scaled, far), near], axis=1)
    outgoing = jnp.dot(row_map, both, preferred_element_type=f32).astype(bf16)
    incoming = lax.all_to_all(
        outgoing.reshape(GRID, SLOTS, 2 * SLICE), ("x", "y"), split_axis=0, concat_axis=0, tiled=True
    ).reshape(ROWS, 2 * SLICE)
    own_rows, other_rows = incoming[:, :SLICE], incoming[:, SLICE:]
    part = (
        jnp.dot(own_rows, gate_up, preferred_element_type=f32)
        + jnp.dot(other_rows, other_gate_up, preferred_element_type=f32)
    ).astype(bf16)
    sums = lax.psum_scatter(part, "h", scatter_dimension=0, tiled=True).astype(f32)
    squares = jnp.sum(
        jnp.square(own_rows.astype(f32)) * inverse
        + jnp.square(other_rows.astype(f32)) * other_inverse,
        axis=1,
    )
    totals = lax.psum(squares, "h")
    totals = lax.dynamic_slice_in_dim(totals, lax.axis_index("h") * SHARE, SHARE, 0)
    sums = sums * lax.rsqrt(totals / D + epsilon)[:, None]
    hidden = (jax.nn.silu(sums[:, :FF]) * sums[:, FF:]).astype(bf16)
    all_hidden = lax.all_gather(hidden, "h", axis=0, tiled=True)
    results = jnp.dot(all_hidden, down, preferred_element_type=f32).astype(bf16)
    returned = lax.all_to_all(
        results.reshape(GRID, SLOTS, 2 * SLICE), ("x", "y"), split_axis=0, concat_axis=0, tiled=True
    ).reshape(ROWS, 2 * SLICE)
    mixed = jnp.einsum("rt,rd->td", combine, returned, preferred_element_type=f32)
    own_mixed, other_mixed = mixed[:, :SLICE], mixed[:, SLICE:].astype(bf16)
    from_near, from_far = cycle_back(other_mixed), across(own_mixed.astype(bf16))
    expert_out = from_near.astype(f32) + jnp.where(core == 0, own_mixed, from_far.astype(f32))
    return stream.astype(bf16), expert_out.astype(bf16)


def solution(mesh):
    split = Mesh(np.asarray(mesh.devices).reshape(NX, NY, NL, NH, NC), ("x", "y", "l", "h", "c"))
    ctx, exp = CTX, ("h", "c")
    placed = (
        P(ctx, exp),
        P(ctx, None),
        P(ctx, None),
        P(ctx, exp),
        P(ctx, exp),
        P(exp),
        P(ctx, exp, None),
        P(ctx, exp, None),
        P(ctx, None, exp),
        P(ctx, None),
        P(ctx, None),
        P(ctx, None),
        P(ctx, None),
        P(ctx),
    )
    return jax.shard_map(
        body,
        mesh=split,
        in_specs=placed,
        out_specs=(P(ctx, exp), P(ctx, exp)),
        check_vma=False,
    )
```

```python
import jax
import jax.numpy as jnp
import numpy as np
from jax import lax
from jax.sharding import Mesh, PartitionSpec as P

D = 4096
HD = 128
TOPK = 8
QH = 32
KVH = 2
FF = 768
FIX = 32
TOK = 128
SLOTS = 21
NX, NY, NL, NH, NC = 4, 8, 2, 4, 2
N_CTX = NX * NY * NL
GRID = NX * NY
ROWS = GRID * SLOTS
SHARE = ROWS // NH
SLICE = D // (NH * NC)
CTX = ("x", "y", "l")
f32, bf16 = jnp.float32, jnp.bfloat16

epsilon = 1e-06


def swap(block, axis):
    return lax.ppermute(block, axis, [(0, 1), (1, 0)])


def exchange(blocks, axes):
    return lax.all_to_all(blocks, axes, split_axis=0, concat_axis=0, tiled=True)


def from_behind(block, distance):
    route = [(i, i + distance) for i in range(N_CTX - distance)]
    return lax.ppermute(block, CTX, route)


def attention(queries, key_rows, value_rows):
    tokens = queries.shape[0]
    block = lax.axis_index(CTX)
    kv_first = lax.axis_index("h") // 2 * HD
    own = jnp.concatenate(
        [
            lax.dynamic_slice_in_dim(key_rows, kv_first, HD, 1),
            lax.dynamic_slice_in_dim(value_rows, kv_first, HD, 1),
        ],
        axis=1,
    )
    pairs = [from_behind(own, 3), from_behind(own, 2), from_behind(own, 1), own]
    keys = jnp.concatenate([pair[:, :HD] for pair in pairs], axis=0)
    values = jnp.concatenate([pair[:, HD:] for pair in pairs], axis=0)
    q_view = queries.reshape(tokens, -1, HD)
    scores = jnp.einsum("tgd,sd->gts", q_view, keys, preferred_element_type=f32) / HD**0.5
    q_pos = block * tokens + jnp.arange(tokens)
    k_pos = (block - 3) * tokens + jnp.arange(4 * tokens)
    allowed = (k_pos[None, :] >= 0) & (k_pos[None, :] <= q_pos[:, None])
    scores = jnp.where(allowed, scores, -1e30)
    highest = jnp.max(scores, axis=2, keepdims=True)
    weights = jnp.where(allowed, jnp.exp(scores - highest), 0.0)
    denominators = jnp.sum(weights, axis=2, keepdims=True)
    mixed = (
        jnp.einsum("gts,sd->gtd", weights.astype(bf16), values, preferred_element_type=f32)
        / denominators
    )
    return jnp.transpose(mixed, (1, 0, 2)).reshape(tokens, -1).astype(bf16)


def slots_of(pred_ids, fix_pair, fix_expert, fix_count):
    tokens = pred_ids.shape[0]
    places = jnp.arange(tokens * TOPK, dtype=jnp.int32).reshape(tokens, TOPK)
    live = jnp.arange(FIX) < fix_count[0]
    hit = (places[:, :, None] == fix_pair[0][None, None, :]) & live[None, None, :]
    fixed = jnp.sum(jnp.where(hit, fix_expert[0][None, None, :], 0), axis=2)
    ids = jnp.where(jnp.any(hit, axis=2), fixed, pred_ids)
    named = ids[:, :, None] == jnp.arange(N_CTX)[None, None, :]
    counts = jnp.sum(named.astype(f32), axis=1)
    earlier = (
        jnp.arange(tokens)[:, None] > jnp.arange(tokens)[None, :]
    ).astype(bf16)
    before = jnp.dot(earlier, counts.astype(bf16), preferred_element_type=f32)
    rank = jnp.sum(jnp.where(named, before[:, None, :], 0.0), axis=2)
    twin = (ids[:, :, None] == ids[:, None, :]) & (
        jnp.arange(TOPK)[None, :, None] > jnp.arange(TOPK)[None, None, :]
    )
    rank = rank + jnp.sum(twin.astype(f32), axis=2)
    return ids.astype(f32), rank


def row_slots(table, side):
    ids, rank, gates = table[:TOPK], table[TOPK : 2 * TOPK], table[2 * TOPK :]
    column = jnp.floor(ids * 0.5)
    return jnp.where(ids - 2.0 * column == side, column * SLOTS + rank, -1.0), gates


def spread(slots, values):
    row_ids = jnp.arange(ROWS, dtype=f32)[:, None]
    total = jnp.zeros((ROWS, slots.shape[1]), f32)
    for k in range(TOPK):
        total = total + jnp.where(slots[k][None, :] == row_ids, values[k][None, :], 0.0)
    return total.astype(bf16)


def body(
    queries,
    key_rows,
    value_rows,
    out_weight,
    residual,
    norm_gain,
    w_gate,
    w_up,
    w_down,
    pred_ids,
    route_gates,
    fix_pair,
    fix_expert,
    fix_count,
):
    core, side = lax.axis_index("c"), lax.axis_index("l")
    tokens = queries.shape[0]
    half = FF // 2

    attended = attention(queries, key_rows, value_rows)

    other_strip = swap(out_weight, "l")
    strips = jnp.concatenate(
        [
            jnp.where(side == 0, out_weight, other_strip),
            jnp.where(side == 0, other_strip, out_weight),
        ],
        axis=0,
    )
    quarter = lax.all_gather(strips, "y", axis=0, tiled=True)

    ids, rank = slots_of(pred_ids, fix_pair, fix_expert, fix_count)
    table = jnp.concatenate([ids, rank, route_gates.astype(f32)], axis=1)
    tables = (table.T, swap(table, "l").T)

    def columns(which):
        return jnp.concatenate(
            [
                lax.dynamic_slice_in_dim(w_gate[0], which * half, half, 1),
                lax.dynamic_slice_in_dim(w_up[0], which * half, half, 1),
            ],
            axis=1,
        )

    gate_up, other_gate_up = columns(core), swap(columns(1 - core), "c")
    down = lax.dynamic_slice_in_dim(w_down[0], core * half, half, 0)
    other_down = lax.dynamic_slice_in_dim(w_down[0], (1 - core) * half, half, 0)
    gain = norm_gain[None, :]
    inverse = 1.0 / (gain * gain)
    other_inverse = swap(inverse, "c")

    copies = jnp.broadcast_to(attended[None], (NH, *attended.shape))
    heads = exchange(exchange(copies, "h"), "x").reshape(NX * tokens, SLICE)
    other_heads = swap(heads, "c")
    partial = jnp.dot(
        heads,
        lax.dynamic_slice_in_dim(quarter, core * SLICE, SLICE, 0),
        preferred_element_type=f32,
    ) + jnp.dot(
        other_heads,
        lax.dynamic_slice_in_dim(quarter, (1 - core) * SLICE, SLICE, 0),
        preferred_element_type=f32,
    )
    terms = exchange(partial.astype(bf16).reshape(NX, tokens, SLICE), "x")
    stream = residual.astype(f32) + jnp.sum(terms.astype(f32), axis=0)

    scaled = (stream * gain).astype(bf16)
    blocks = (scaled, swap(scaled, "l"))
    mixed = []
    for table, rows in zip(tables, blocks):
        slots, gates = row_slots(table, side.astype(f32))
        outgoing = jnp.dot(
            spread(slots, jnp.ones_like(gates)), rows, preferred_element_type=f32
        ).astype(bf16)
        incoming = exchange(outgoing.reshape(GRID, SLOTS, SLICE), ("x", "y")).reshape(ROWS, SLICE)
        other_incoming = swap(incoming, "c")
        part = (
            jnp.dot(incoming, gate_up, preferred_element_type=f32)
            + jnp.dot(other_incoming, other_gate_up, preferred_element_type=f32)
        ).astype(bf16)
        squares = jnp.sum(
            jnp.square(incoming.astype(f32)) * inverse
            + jnp.square(other_incoming.astype(f32)) * other_inverse,
            axis=1,
        ).reshape(NH, 1, SHARE)
        high = squares.astype(bf16)
        low = (squares - high.astype(f32)).astype(bf16)
        extra = jnp.pad(jnp.concatenate([high, low], axis=1), ((0, 0), (0, 6), (0, FF - SHARE)))
        parts = exchange(
            jnp.concatenate([part.reshape(NH, SHARE, FF), extra], axis=1), "h"
        ).astype(f32)
        sums = jnp.sum(parts[:, :SHARE], axis=0)
        total = jnp.sum(parts[:, SHARE : SHARE + 2, :SHARE], axis=(0, 1))
        sums = sums * lax.rsqrt(total / D + epsilon)[:, None]
        hidden = (jax.nn.silu(sums[:, :half]) * sums[:, half:]).astype(bf16)
        copies = jnp.broadcast_to(hidden[None], (NH, SHARE, half))
        all_hidden = exchange(copies, "h").reshape(ROWS, half)
        other_hidden = swap(all_hidden, "c")
        results = (
            jnp.dot(all_hidden, down, preferred_element_type=f32)
            + jnp.dot(other_hidden, other_down, preferred_element_type=f32)
        ).astype(bf16)
        returned = exchange(results.reshape(GRID, SLOTS, SLICE), ("x", "y")).reshape(ROWS, SLICE)
        mixed.append(
            jnp.einsum("rt,rd->td", spread(slots, gates), returned, preferred_element_type=f32)
        )
    expert_out = mixed[0] + swap(mixed[1].astype(bf16), "l").astype(f32)
    return stream.astype(bf16), expert_out.astype(bf16)


def solution(mesh):
    split = Mesh(np.asarray(mesh.devices).reshape(NX, NY, NL, NH, NC), ("x", "y", "l", "h", "c"))
    ctx, exp = CTX, ("h", "c")
    placed = (
        P(ctx, exp),
        P(ctx, None),
        P(ctx, None),
        P(ctx, exp),
        P(ctx, exp),
        P(exp),
        P(ctx, exp, None),
        P(ctx, exp, None),
        P(ctx, None, exp),
        P(ctx, None),
        P(ctx, None),
        P(ctx, None),
        P(ctx, None),
        P(ctx),
    )
    return jax.shard_map(
        body,
        mesh=split,
        in_specs=placed,
        out_specs=(P(ctx, exp), P(ctx, exp)),
        check_vma=False,
    )
```

```python
import jax
import jax.numpy as jnp
import numpy as np
from jax import lax
from jax.experimental import pallas as pl
from jax.experimental.pallas import tpu as pltpu
from jax.sharding import Mesh, PartitionSpec as P

D = 4096
HD = 128
TOPK = 8
QH = 32
KVH = 2
FF = 768
FIX = 32
TOK = 128
SLOTS = 21
GROUP = 24
NX, NY, NL, NH, NC = 4, 8, 2, 4, 2
N_CTX = NX * NY * NL
GRID = NX * NY
ROWS = GRID * GROUP
SHARE = ROWS // NH
SLICE = D // (NH * NC)
CTX = ("x", "y", "l")
f32, bf16 = jnp.float32, jnp.bfloat16

epsilon = 1e-06


def swap(block, axis):
    return lax.ppermute(block, axis, [(0, 1), (1, 0)])


def exchange(blocks, axes):
    return lax.all_to_all(blocks, axes, split_axis=0, concat_axis=0, tiled=True)


def from_behind(block, distance):
    route = [(i, i + distance) for i in range(N_CTX - distance)]
    return lax.ppermute(block, CTX, route)


def attention(queries, key_rows, value_rows):
    tokens = queries.shape[0]
    block = lax.axis_index(CTX)
    kv_first = lax.axis_index("h") // 2 * HD
    own = jnp.concatenate(
        [
            lax.dynamic_slice_in_dim(key_rows, kv_first, HD, 1),
            lax.dynamic_slice_in_dim(value_rows, kv_first, HD, 1),
        ],
        axis=1,
    )
    pairs = [from_behind(own, 3), from_behind(own, 2), from_behind(own, 1), own]
    keys = jnp.concatenate([pair[:, :HD] for pair in pairs], axis=0)
    values = jnp.concatenate([pair[:, HD:] for pair in pairs], axis=0)
    q_view = queries.reshape(tokens, -1, HD)
    scores = jnp.einsum("tgd,sd->gts", q_view, keys, preferred_element_type=f32) / HD**0.5
    q_pos = block * tokens + jnp.arange(tokens)
    k_pos = (block - 3) * tokens + jnp.arange(4 * tokens)
    allowed = (k_pos[None, :] >= 0) & (k_pos[None, :] <= q_pos[:, None])
    scores = jnp.where(allowed, scores, -1e30)
    highest = jnp.max(scores, axis=2, keepdims=True)
    weights = jnp.where(allowed, jnp.exp(scores - highest), 0.0)
    denominators = jnp.sum(weights, axis=2, keepdims=True)
    mixed = (
        jnp.einsum("gts,sd->gtd", weights.astype(bf16), values, preferred_element_type=f32)
        / denominators
    )
    return jnp.transpose(mixed, (1, 0, 2)).reshape(tokens, -1).astype(bf16)


def slots_of(pred_ids, fix_pair, fix_expert, fix_count):
    tokens = pred_ids.shape[0]
    places = jnp.arange(tokens * TOPK, dtype=jnp.int32).reshape(tokens, TOPK)
    live = jnp.arange(FIX) < fix_count[0]
    hit = (places[:, :, None] == fix_pair[0][None, None, :]) & live[None, None, :]
    fixed = jnp.sum(jnp.where(hit, fix_expert[0][None, None, :], 0), axis=2)
    ids = jnp.where(jnp.any(hit, axis=2), fixed, pred_ids)
    named = ids[:, :, None] == jnp.arange(N_CTX)[None, None, :]
    counts = jnp.sum(named.astype(f32), axis=1)
    earlier = (
        jnp.arange(tokens)[:, None] > jnp.arange(tokens)[None, :]
    ).astype(bf16)
    before = jnp.dot(earlier, counts.astype(bf16), preferred_element_type=f32)
    rank = jnp.sum(jnp.where(named, before[:, None, :], 0.0), axis=2)
    twin = (ids[:, :, None] == ids[:, None, :]) & (
        jnp.arange(TOPK)[None, :, None] > jnp.arange(TOPK)[None, None, :]
    )
    rank = rank + jnp.sum(twin.astype(f32), axis=2)
    return ids.astype(f32), rank


def row_slots(table, side):
    ids, rank, gates = table[:TOPK], table[TOPK : 2 * TOPK], table[2 * TOPK :]
    column = jnp.floor(ids * 0.5)
    return jnp.where(ids - 2.0 * column == side, column * GROUP + rank, -1.0), gates


def spread(slots, values):
    row_ids = jnp.arange(ROWS, dtype=f32)[:, None]
    total = jnp.zeros((ROWS, slots.shape[1]), f32)
    for k in range(TOPK):
        total = total + jnp.where(slots[k][None, :] == row_ids, values[k][None, :], 0.0)
    return total.astype(bf16)


def products_kernel(own_ref, other_ref, w_own_ref, w_other_ref, inv_own_ref, inv_other_ref, out_ref):
    own, other = own_ref[...], other_ref[...]
    w_own, w_other = w_own_ref[...], w_other_ref[...]

    def squares(rows, inverse_ref):
        weight = jnp.broadcast_to(inverse_ref[...], (8, SLICE))
        return lax.dot_general(
            weight,
            jnp.square(rows.astype(f32)),
            (((1,), (1,)), ((), ())),
            precision=lax.Precision.HIGHEST,
            preferred_element_type=f32,
        )

    total = (squares(own, inv_own_ref) + squares(other, inv_other_ref))[:1]
    high = total.astype(bf16).astype(f32)
    low = total - high
    row = lax.broadcasted_iota(jnp.int32, (16, FF), 0)
    for h in range(NH):
        rows = slice(h * SHARE, (h + 1) * SHARE)
        part = jnp.dot(own[rows], w_own, preferred_element_type=f32) + jnp.dot(
            other[rows], w_other, preferred_element_type=f32
        )
        out_ref[h] = part.astype(bf16)
        tile = jnp.where(row == SLOTS - 16, high, part[16:32])
        tile = jnp.where(row == SLOTS - 15, low, tile)
        out_ref[h, 16:32] = tile.astype(bf16)


def products(own, other, w_own, w_other, inv_own, inv_other):
    return pl.pallas_call(
        products_kernel,
        out_shape=jax.ShapeDtypeStruct((NH, SHARE, FF), bf16),
        compiler_params=pltpu.CompilerParams(vmem_limit_bytes=48 * 1024 * 1024),
        cost_estimate=pl.CostEstimate(
            flops=100_000_000, bytes_accessed=500_000, transcendentals=0
        ),
    )(own, other, w_own, w_other, inv_own, inv_other)


def to_ahead(block, distance):
    return lax.ppermute(block, "h", [(i, (i + distance) % NH) for i in range(NH)])


def body(
    queries,
    key_rows,
    value_rows,
    out_weight,
    residual,
    norm_gain,
    w_gate,
    w_up,
    w_down,
    pred_ids,
    route_gates,
    fix_pair,
    fix_expert,
    fix_count,
):
    core, side, level = lax.axis_index("c"), lax.axis_index("l"), lax.axis_index("h")
    tokens = queries.shape[0]
    half = FF // 2

    attended = attention(queries, key_rows, value_rows)

    other_strip = swap(out_weight, "l")
    strips = jnp.concatenate(
        [
            jnp.where(side == 0, out_weight, other_strip),
            jnp.where(side == 0, other_strip, out_weight),
        ],
        axis=0,
    )
    quarter = lax.all_gather(strips, "y", axis=0, tiled=True)

    ids, rank = slots_of(pred_ids, fix_pair, fix_expert, fix_count)
    table = jnp.concatenate([ids, rank, route_gates.astype(f32)], axis=1)
    tables = (table.T, swap(table, "l").T)

    def columns(which):
        return jnp.concatenate(
            [
                lax.dynamic_slice_in_dim(w_gate[0], which * half, half, 1),
                lax.dynamic_slice_in_dim(w_up[0], which * half, half, 1),
            ],
            axis=1,
        )

    gate_up, other_gate_up = columns(core), swap(columns(1 - core), "c")
    down = lax.dynamic_slice_in_dim(w_down[0], core * half, half, 0)
    other_down = lax.dynamic_slice_in_dim(w_down[0], (1 - core) * half, half, 0)
    gain = norm_gain[None, :]
    inverse = 1.0 / (gain * gain)
    other_inverse = swap(inverse, "c")

    copies = jnp.broadcast_to(attended[None], (NH, *attended.shape))
    heads = exchange(exchange(copies, "h"), "x").reshape(NX * tokens, SLICE)
    heads, gate_up, other_gate_up, inverse, other_inverse, tables = lax.optimization_barrier(
        (heads, gate_up, other_gate_up, inverse, other_inverse, tables)
    )
    other_heads = swap(heads, "c")
    partial = jnp.dot(
        heads,
        lax.dynamic_slice_in_dim(quarter, core * SLICE, SLICE, 0),
        preferred_element_type=f32,
    ) + jnp.dot(
        other_heads,
        lax.dynamic_slice_in_dim(quarter, (1 - core) * SLICE, SLICE, 0),
        preferred_element_type=f32,
    )
    terms = exchange(partial.astype(bf16).reshape(NX, tokens, SLICE), "x")
    stream = residual.astype(f32) + jnp.sum(terms.astype(f32), axis=0)

    scaled = (stream * gain).astype(bf16)
    slot_lists = [row_slots(table, side.astype(f32)) for table in tables]
    def chosen(slot_list, rows):
        slots, gates = slot_list
        picks = spread(slots, jnp.ones_like(gates))
        return jnp.dot(picks, rows, preferred_element_type=f32).astype(bf16)

    def through(rows):
        return exchange(rows.reshape(GRID, GROUP, SLICE), ("x", "y")).reshape(ROWS, SLICE)

    def share_products(rows):
        return products(rows, swap(rows, "c"), gate_up, other_gate_up, inverse, other_inverse)

    def scattered(parts):
        flat = parts.reshape(ROWS, FF)
        return lax.psum_scatter(flat, "h", scatter_dimension=0, tiled=True).astype(f32)

    def activated(sums):
        total = lax.dynamic_slice_in_dim(
            jnp.sum(sums[SLOTS : SLOTS + 2], axis=0), level * SHARE, SHARE, 0
        )
        used = jnp.arange(SHARE) % GROUP < SLOTS
        sums = jnp.where(
            used[:, None], sums * lax.rsqrt(total / D + epsilon)[:, None], 0.0
        )
        return (jax.nn.silu(sums[:, :half]) * sums[:, half:]).astype(bf16)

    def gathered(hidden):
        every = jnp.zeros((NH, SHARE, half), bf16)
        every = lax.dynamic_update_index_in_dim(every, hidden, level, 0)
        for distance in (2, 1, 3):
            every = lax.dynamic_update_index_in_dim(
                every, to_ahead(hidden, distance), (level - distance) % NH, 0
            )
        return every.reshape(ROWS, half)

    def finished(hidden):
        return (
            jnp.dot(hidden, down, preferred_element_type=f32)
            + jnp.dot(swap(hidden, "c"), other_down, preferred_element_type=f32)
        ).astype(bf16)

    def combined(slot_list, returned):
        return jnp.einsum("rt,rd->td", spread(*slot_list), returned, preferred_element_type=f32)

    beside = swap(scaled, "l")
    first = share_products(through(chosen(slot_lists[0], scaled)))
    first, beside = lax.optimization_barrier((first, beside))
    second = share_products(through(chosen(slot_lists[1], beside)))
    parts = exchange(second, "h")
    first = finished(gathered(activated(scattered(first))))
    first, parts = lax.optimization_barrier((first, parts))
    first = through(first)
    hidden = gathered(activated(jnp.sum(parts.astype(f32), axis=0)))
    first, hidden = lax.optimization_barrier((first, hidden))
    second = through(finished(hidden))
    mixed = combined(slot_lists[0], first)
    other_mixed = combined(slot_lists[1], second)
    expert_out = mixed + swap(other_mixed.astype(bf16), "l").astype(f32)
    return stream.astype(bf16), expert_out.astype(bf16)


def solution(mesh):
    split = Mesh(np.asarray(mesh.devices).reshape(NX, NY, NL, NH, NC), ("x", "y", "l", "h", "c"))
    ctx, exp = CTX, ("h", "c")
    placed = (
        P(ctx, exp),
        P(ctx, None),
        P(ctx, None),
        P(ctx, exp),
        P(ctx, exp),
        P(exp),
        P(ctx, exp, None),
        P(ctx, exp, None),
        P(ctx, None, exp),
        P(ctx, None),
        P(ctx, None),
        P(ctx, None),
        P(ctx, None),
        P(ctx),
    )
    return jax.shard_map(
        body,
        mesh=split,
        in_specs=placed,
        out_specs=(P(ctx, exp), P(ctx, exp)),
        check_vma=False,
    )
```

```python
import jax
import jax.numpy as jnp
import numpy as np
from jax import lax
from jax.experimental import pallas as pl
from jax.experimental.pallas import tpu as pltpu
from jax.sharding import Mesh, PartitionSpec as P

D = 4096
HD = 128
TOPK = 8
QH = 32
KVH = 2
FF = 768
FIX = 32
TOK = 128
SLOTS = 21
GROUP = 24
NX, NY, NL, NH, NC = 4, 8, 2, 4, 2
N_CTX = NX * NY * NL
SENT = N_CTX * GROUP
ROWS = N_CTX * SLOTS
SHARE = ROWS // NH
PACK = 8 * SLOTS
PACK_SENT = 8 * GROUP
SLICE = D // (NH * NC)
CTX = ("x", "y", "l")
f32, bf16 = jnp.float32, jnp.bfloat16

epsilon = 1e-06


def swap(block, axis):
    return lax.ppermute(block, axis, [(0, 1), (1, 0)])


def exchange(blocks, axes):
    return lax.all_to_all(blocks, axes, split_axis=0, concat_axis=0, tiled=True)


def from_behind(block, distance):
    route = [(i, i + distance) for i in range(N_CTX - distance)]
    return lax.ppermute(block, CTX, route)


def attention(queries, key_rows, value_rows):
    tokens = queries.shape[0]
    block = lax.axis_index(CTX)
    kv_first = lax.axis_index("h") // 2 * HD
    own = jnp.concatenate(
        [
            lax.dynamic_slice_in_dim(key_rows, kv_first, HD, 1),
            lax.dynamic_slice_in_dim(value_rows, kv_first, HD, 1),
        ],
        axis=1,
    )
    pairs = [from_behind(own, 3), from_behind(own, 2), from_behind(own, 1), own]
    keys = jnp.concatenate([pair[:, :HD] for pair in pairs], axis=0)
    values = jnp.concatenate([pair[:, HD:] for pair in pairs], axis=0)
    q_view = queries.reshape(tokens, -1, HD)
    scores = jnp.einsum("tgd,sd->gts", q_view, keys, preferred_element_type=f32) / HD**0.5
    q_pos = block * tokens + jnp.arange(tokens)
    k_pos = (block - 3) * tokens + jnp.arange(4 * tokens)
    allowed = (k_pos[None, :] >= 0) & (k_pos[None, :] <= q_pos[:, None])
    scores = jnp.where(allowed, scores, -1e30)
    highest = jnp.max(scores, axis=2, keepdims=True)
    weights = jnp.where(allowed, jnp.exp(scores - highest), 0.0)
    denominators = jnp.sum(weights, axis=2, keepdims=True)
    mixed = (
        jnp.einsum("gts,sd->gtd", weights.astype(bf16), values, preferred_element_type=f32)
        / denominators
    )
    return jnp.transpose(mixed, (1, 0, 2)).reshape(tokens, -1).astype(bf16)


def slots_of(pred_ids, fix_pair, fix_expert, fix_count):
    tokens = pred_ids.shape[0]
    places = jnp.arange(tokens * TOPK, dtype=jnp.int32).reshape(tokens, TOPK)
    live = jnp.arange(FIX) < fix_count[0]
    hit = (places[:, :, None] == fix_pair[0][None, None, :]) & live[None, None, :]
    fixed = jnp.sum(jnp.where(hit, fix_expert[0][None, None, :], 0), axis=2)
    ids = jnp.where(jnp.any(hit, axis=2), fixed, pred_ids)
    named = ids[:, :, None] == jnp.arange(N_CTX)[None, None, :]
    counts = jnp.sum(named.astype(f32), axis=1)
    earlier = (
        jnp.arange(tokens)[:, None] > jnp.arange(tokens)[None, :]
    ).astype(bf16)
    before = jnp.dot(earlier, counts.astype(bf16), preferred_element_type=f32)
    rank = jnp.sum(jnp.where(named, before[:, None, :], 0.0), axis=2)
    twin = (ids[:, :, None] == ids[:, None, :]) & (
        jnp.arange(TOPK)[None, :, None] > jnp.arange(TOPK)[None, None, :]
    )
    rank = rank + jnp.sum(twin.astype(f32), axis=2)
    return ids.astype(f32), rank


def spread(slots, values):
    row_ids = jnp.arange(SENT, dtype=f32)[:, None]
    total = jnp.zeros((SENT, slots.shape[1]), f32)
    for k in range(TOPK):
        total = total + jnp.where(slots[k][None, :] == row_ids, values[k][None, :], 0.0)
    return total.astype(bf16)


def packing():
    place = np.arange(PACK)
    return (place // SLOTS * GROUP + place % SLOTS)[:, None] == np.arange(PACK_SENT)[None, :]


def products_kernel(
    own_ref, other_ref, w_own_ref, w_other_ref, inv_own_ref, inv_other_ref, pick_ref, gate_ref, up_ref
):
    half = FF // 2
    pick = pick_ref[...]
    ones = jnp.ones((8, SLICE), bf16)

    def packed(ref, h):
        first, second = (
            jnp.dot(
                pick,
                ref[(2 * h + i) * PACK_SENT : (2 * h + i + 1) * PACK_SENT],
                preferred_element_type=f32,
            )
            for i in range(2)
        )
        return jnp.concatenate([first, second], axis=0)

    def squares(rows, inverse_ref):
        weighted = jnp.concatenate(
            [rows * rows * inverse_ref[...], jnp.zeros((half - SHARE, SLICE), f32)], axis=0
        )
        high = weighted.astype(bf16)
        low = (weighted - high.astype(f32)).astype(bf16)
        across = (((1,), (1,)), ((), ()))
        return lax.dot_general(ones, high, across, preferred_element_type=f32) + lax.dot_general(
            ones, low, across, preferred_element_type=f32
        )

    row = lax.broadcasted_iota(jnp.int32, (16, half), 0)
    for h in range(NH):
        own, other = packed(own_ref, h), packed(other_ref, h)
        part = jnp.dot(own.astype(bf16), w_own_ref[...], preferred_element_type=f32) + jnp.dot(
            other.astype(bf16), w_other_ref[...], preferred_element_type=f32
        )
        gate_ref[h] = part[:, :half].astype(bf16)
        up_ref[h, :SHARE] = part[:, half:].astype(bf16)
        total = (squares(own, inv_own_ref) + squares(other, inv_other_ref))[:1]
        high = total.astype(bf16).astype(f32)
        tile = jnp.where(row == 0, high, jnp.where(row == 1, total - high, 0.0))
        up_ref[h, SHARE:] = tile.astype(bf16)


def products(own, other, w_own, w_other, inv_own, inv_other):
    half = FF // 2
    return pl.pallas_call(
        products_kernel,
        out_shape=(
            jax.ShapeDtypeStruct((NH, SHARE, half), bf16),
            jax.ShapeDtypeStruct((NH, SHARE + 16, half), bf16),
        ),
        compiler_params=pltpu.CompilerParams(vmem_limit_bytes=48 * 1024 * 1024),
        cost_estimate=pl.CostEstimate(flops=100_000_000, bytes_accessed=500_000, transcendentals=0),
    )(own, other, w_own, w_other, inv_own, inv_other, jnp.asarray(packing(), bf16))


def results_kernel(own_ref, other_ref, down_own_ref, down_other_ref, place_ref, out_ref):
    place = place_ref[...]
    for h in range(NH):
        rows = slice(h * SHARE, (h + 1) * SHARE)
        part = jnp.dot(own_ref[rows], down_own_ref[...], preferred_element_type=f32) + jnp.dot(
            other_ref[rows], down_other_ref[...], preferred_element_type=f32
        )
        for i in range(2):
            rows = part[i * PACK : (i + 1) * PACK].astype(bf16)
            start = (2 * h + i) * PACK_SENT
            out_ref[start : start + PACK_SENT] = jnp.dot(
                place, rows, preferred_element_type=f32
            ).astype(bf16)


def expert_results(own, other, down_own, down_other):
    return pl.pallas_call(
        results_kernel,
        out_shape=jax.ShapeDtypeStruct((SENT, SLICE), bf16),
        compiler_params=pltpu.CompilerParams(vmem_limit_bytes=48 * 1024 * 1024),
        cost_estimate=pl.CostEstimate(flops=100_000_000, bytes_accessed=500_000, transcendentals=0),
    )(own, other, down_own, down_other, jnp.asarray(packing().T, bf16))


def body(
    queries,
    key_rows,
    value_rows,
    out_weight,
    residual,
    norm_gain,
    w_gate,
    w_up,
    w_down,
    pred_ids,
    route_gates,
    fix_pair,
    fix_expert,
    fix_count,
):
    core, side = lax.axis_index("c"), lax.axis_index("l")
    tokens = queries.shape[0]
    half = FF // 2

    other_strip = swap(out_weight, "l")
    strips = jnp.concatenate(
        [
            jnp.where(side == 0, out_weight, other_strip),
            jnp.where(side == 0, other_strip, out_weight),
        ],
        axis=0,
    )
    strips, queries = lax.optimization_barrier((strips, queries))
    quarter = lax.all_gather(strips, "y", axis=0, tiled=True)

    attended = attention(queries, key_rows, value_rows)
    attended, w_gate, w_up, norm_gain, pred_ids = lax.optimization_barrier(
        (attended, w_gate, w_up, norm_gain, pred_ids)
    )

    ids, rank = slots_of(pred_ids, fix_pair, fix_expert, fix_count)
    slots, gates = (ids * GROUP + rank).T, route_gates.astype(f32).T

    def columns(which):
        return jnp.concatenate(
            [
                lax.dynamic_slice_in_dim(w_gate[0], which * half, half, 1),
                lax.dynamic_slice_in_dim(w_up[0], which * half, half, 1),
            ],
            axis=1,
        )

    gate_up, other_gate_up = columns(core), swap(columns(1 - core), "c")
    down = lax.dynamic_slice_in_dim(w_down[0], core * half, half, 0)
    other_down = lax.dynamic_slice_in_dim(w_down[0], (1 - core) * half, half, 0)
    gain = norm_gain[None, :]
    inverse = 1.0 / (gain * gain)
    other_inverse = swap(inverse, "c")

    copies = jnp.broadcast_to(attended[None], (NH, *attended.shape))
    heads = exchange(exchange(copies, "h"), "x").reshape(NX * tokens, SLICE)
    heads, gate_up, other_gate_up, inverse, other_inverse, slots = lax.optimization_barrier(
        (heads, gate_up, other_gate_up, inverse, other_inverse, slots)
    )
    other_heads = swap(heads, "c")
    partial = jnp.dot(
        heads,
        lax.dynamic_slice_in_dim(quarter, core * SLICE, SLICE, 0),
        preferred_element_type=f32,
    ) + jnp.dot(
        other_heads,
        lax.dynamic_slice_in_dim(quarter, (1 - core) * SLICE, SLICE, 0),
        preferred_element_type=f32,
    )
    terms = exchange(partial.astype(bf16).reshape(NX, tokens, SLICE), "x")
    stream = residual.astype(f32) + jnp.sum(terms.astype(f32), axis=0)

    scaled = (stream * gain).astype(bf16)
    picks = spread(slots, jnp.ones_like(gates))
    outgoing = jnp.dot(picks, scaled, preferred_element_type=f32).astype(bf16)
    incoming = exchange(outgoing.reshape(N_CTX, GROUP, SLICE), CTX).reshape(SENT, SLICE)
    gate_part, up_part = products(
        incoming, swap(incoming, "c"), gate_up, other_gate_up, inverse, other_inverse
    )
    gate_sum = lax.psum_scatter(
        gate_part.reshape(ROWS, half), "h", scatter_dimension=0, tiled=True
    ).astype(f32)
    up_sum = jnp.sum(exchange(up_part, "h").astype(f32), axis=0)
    total = jnp.sum(up_sum[SHARE:], axis=0)[:SHARE]
    scale = lax.rsqrt(total / D + epsilon)[:, None]
    hidden = (jax.nn.silu(gate_sum * scale) * (up_sum[:SHARE] * scale)).astype(bf16)
    all_hidden = lax.all_gather(hidden, "h", axis=0, tiled=True)
    results = expert_results(all_hidden, swap(all_hidden, "c"), down, other_down)
    returned = exchange(results.reshape(N_CTX, GROUP, SLICE), CTX).reshape(SENT, SLICE)
    expert_out = jnp.einsum("rt,rd->td", spread(slots, gates), returned, preferred_element_type=f32)
    return stream.astype(bf16), expert_out.astype(bf16)


def solution(mesh):
    split = Mesh(np.asarray(mesh.devices).reshape(NX, NY, NL, NH, NC), ("x", "y", "l", "h", "c"))
    ctx, exp = CTX, ("h", "c")
    placed = (
        P(ctx, exp),
        P(ctx, None),
        P(ctx, None),
        P(ctx, exp),
        P(ctx, exp),
        P(exp),
        P(ctx, exp, None),
        P(ctx, exp, None),
        P(ctx, None, exp),
        P(ctx, None),
        P(ctx, None),
        P(ctx, None),
        P(ctx, None),
        P(ctx),
    )
    return jax.shard_map(
        body,
        mesh=split,
        in_specs=placed,
        out_specs=(P(ctx, exp), P(ctx, exp)),
        check_vma=False,
    )
```

```python
import jax
import jax.numpy as jnp
import numpy as np
from jax import lax
from jax.experimental import pallas as pl
from jax.experimental.pallas import tpu as pltpu
from jax.sharding import Mesh, PartitionSpec as P

D = 4096
HD = 128
TOPK = 8
QH = 32
KVH = 2
FF = 768
FIX = 32
TOK = 128
SLOTS = 21
GROUP = 24
NX, NY, NL, NH, NC = 4, 8, 2, 4, 2
N_CTX = NX * NY * NL
SENT = N_CTX * GROUP
ROWS = N_CTX * SLOTS
SHARE = ROWS // NH
LANES = 384
PACK = 8 * SLOTS
PACK_SENT = 8 * GROUP
SLICE = D // (NH * NC)
CTX = ("x", "y", "l")
f32, bf16 = jnp.float32, jnp.bfloat16

epsilon = 1e-06


def swap(block, axis):
    return lax.ppermute(block, axis, [(0, 1), (1, 0)])


def exchange(blocks, axes):
    return lax.all_to_all(blocks, axes, split_axis=0, concat_axis=0, tiled=True)


def from_behind(block, distance):
    route = [(i, i + distance) for i in range(N_CTX - distance)]
    return lax.ppermute(block, CTX, route)


def attention(queries, key_rows, value_rows):
    tokens = queries.shape[0]
    block = lax.axis_index(CTX)
    kv_first = lax.axis_index("h") // 2 * HD
    own = jnp.concatenate(
        [
            lax.dynamic_slice_in_dim(key_rows, kv_first, HD, 1),
            lax.dynamic_slice_in_dim(value_rows, kv_first, HD, 1),
        ],
        axis=1,
    )
    pairs = [from_behind(own, 3), from_behind(own, 2), from_behind(own, 1), own]
    keys = jnp.concatenate([pair[:, :HD] for pair in pairs], axis=0)
    values = jnp.concatenate([pair[:, HD:] for pair in pairs], axis=0)
    q_view = queries.reshape(tokens, -1, HD)
    scores = jnp.einsum("tgd,sd->gts", q_view, keys, preferred_element_type=f32) / HD**0.5
    q_pos = block * tokens + jnp.arange(tokens)
    k_pos = (block - 3) * tokens + jnp.arange(4 * tokens)
    allowed = (k_pos[None, :] >= 0) & (k_pos[None, :] <= q_pos[:, None])
    scores = jnp.where(allowed, scores, -1e30)
    highest = jnp.max(scores, axis=2, keepdims=True)
    weights = jnp.where(allowed, jnp.exp(scores - highest), 0.0)
    denominators = jnp.sum(weights, axis=2, keepdims=True)
    mixed = (
        jnp.einsum("gts,sd->gtd", weights.astype(bf16), values, preferred_element_type=f32)
        / denominators
    )
    return jnp.transpose(mixed, (1, 0, 2)).reshape(tokens, -1).astype(bf16)


def slots_of(pred_ids, fix_pair, fix_expert, fix_count):
    tokens = pred_ids.shape[0]
    places = jnp.arange(tokens * TOPK, dtype=jnp.int32).reshape(tokens, TOPK)
    live = jnp.arange(FIX) < fix_count[0]
    hit = (places[:, :, None] == fix_pair[0][None, None, :]) & live[None, None, :]
    fixed = jnp.sum(jnp.where(hit, fix_expert[0][None, None, :], 0), axis=2)
    ids = jnp.where(jnp.any(hit, axis=2), fixed, pred_ids)
    named = ids[:, :, None] == jnp.arange(N_CTX)[None, None, :]
    counts = jnp.sum(named.astype(f32), axis=1)
    earlier = (
        jnp.arange(tokens)[:, None] > jnp.arange(tokens)[None, :]
    ).astype(bf16)
    before = jnp.dot(earlier, counts.astype(bf16), preferred_element_type=f32)
    rank = jnp.sum(jnp.where(named, before[:, None, :], 0.0), axis=2)
    twin = (ids[:, :, None] == ids[:, None, :]) & (
        jnp.arange(TOPK)[None, :, None] > jnp.arange(TOPK)[None, None, :]
    )
    rank = rank + jnp.sum(twin.astype(f32), axis=2)
    return ids.astype(f32), rank


def spread(slots, values):
    row_ids = jnp.arange(SENT, dtype=f32)[:, None]
    total = jnp.zeros((SENT, slots.shape[1]), f32)
    for k in range(TOPK):
        total = total + jnp.where(slots[k][None, :] == row_ids, values[k][None, :], 0.0)
    return total.astype(bf16)


def packing():
    place = np.arange(PACK)
    return (place // SLOTS * GROUP + place % SLOTS)[:, None] == np.arange(PACK_SENT)[None, :]


def products_kernel(
    own_ref, other_ref, w_own_ref, w_other_ref, inv_own_ref, inv_other_ref, pick_ref, part_ref, total_ref
):
    pick = pick_ref[...]
    ones = jnp.ones((8, SLICE), bf16)
    blank = jnp.zeros((LANES - SHARE, SLICE), bf16)

    def packed(ref, h):
        first, second = (
            jnp.dot(
                pick,
                ref[(2 * h + i) * PACK_SENT : (2 * h + i + 1) * PACK_SENT],
                preferred_element_type=f32,
            )
            for i in range(2)
        )
        return jnp.concatenate([first, second], axis=0)

    def squares(rows, inverse_ref):
        weighted = (rows * rows * inverse_ref[...]).astype(bf16)
        return lax.dot_general(
            ones,
            jnp.concatenate([weighted, blank], axis=0),
            (((1,), (1,)), ((), ())),
            preferred_element_type=f32,
        )

    for h in range(NH):
        own, other = packed(own_ref, h), packed(other_ref, h)
        part = jnp.dot(own.astype(bf16), w_own_ref[...], preferred_element_type=f32) + jnp.dot(
            other.astype(bf16), w_other_ref[...], preferred_element_type=f32
        )
        part_ref[h] = part.astype(bf16)
        total_ref[h] = squares(own, inv_own_ref) + squares(other, inv_other_ref)


def products(own, other, w_own, w_other, inv_own, inv_other):
    return pl.pallas_call(
        products_kernel,
        out_shape=(
            jax.ShapeDtypeStruct((NH, SHARE, FF), bf16),
            jax.ShapeDtypeStruct((NH, 8, LANES), f32),
        ),
        compiler_params=pltpu.CompilerParams(vmem_limit_bytes=48 * 1024 * 1024),
        cost_estimate=pl.CostEstimate(flops=100_000_000, bytes_accessed=500_000, transcendentals=0),
    )(own, other, w_own, w_other, inv_own, inv_other, jnp.asarray(packing(), bf16))


def results_kernel(own_ref, other_ref, down_own_ref, down_other_ref, place_ref, out_ref):
    place = place_ref[...]
    for h in range(NH):
        rows = slice(h * SHARE, (h + 1) * SHARE)
        part = jnp.dot(own_ref[rows], down_own_ref[...], preferred_element_type=f32) + jnp.dot(
            other_ref[rows], down_other_ref[...], preferred_element_type=f32
        )
        for i in range(2):
            rows = part[i * PACK : (i + 1) * PACK].astype(bf16)
            start = (2 * h + i) * PACK_SENT
            out_ref[start : start + PACK_SENT] = jnp.dot(
                place, rows, preferred_element_type=f32
            ).astype(bf16)


def expert_results(own, other, down_own, down_other):
    return pl.pallas_call(
        results_kernel,
        out_shape=jax.ShapeDtypeStruct((SENT, SLICE), bf16),
        compiler_params=pltpu.CompilerParams(vmem_limit_bytes=48 * 1024 * 1024),
        cost_estimate=pl.CostEstimate(flops=100_000_000, bytes_accessed=500_000, transcendentals=0),
    )(own, other, down_own, down_other, jnp.asarray(packing().T, bf16))


def body(
    queries,
    key_rows,
    value_rows,
    out_weight,
    residual,
    norm_gain,
    w_gate,
    w_up,
    w_down,
    pred_ids,
    route_gates,
    fix_pair,
    fix_expert,
    fix_count,
):
    core, side = lax.axis_index("c"), lax.axis_index("l")
    tokens = queries.shape[0]
    half = FF // 2

    other_strip = swap(out_weight, "l")
    strips = jnp.concatenate(
        [
            jnp.where(side == 0, out_weight, other_strip),
            jnp.where(side == 0, other_strip, out_weight),
        ],
        axis=0,
    )
    strips, queries = lax.optimization_barrier((strips, queries))
    quarter = lax.all_gather(strips, "y", axis=0, tiled=True)

    attended = attention(queries, key_rows, value_rows)
    heads = lax.all_gather(attended, "h", axis=0, tiled=True).reshape(NH, tokens, SLICE)
    heads, w_gate, w_up, norm_gain, pred_ids, fix_pair = lax.optimization_barrier(
        (heads, w_gate, w_up, norm_gain, pred_ids, fix_pair)
    )

    ids, rank = slots_of(pred_ids, fix_pair, fix_expert, fix_count)
    slots = (ids * GROUP + rank).T

    def columns(which):
        return jnp.concatenate(
            [
                lax.dynamic_slice_in_dim(w_gate[0], which * half, half, 1),
                lax.dynamic_slice_in_dim(w_up[0], which * half, half, 1),
            ],
            axis=1,
        )

    gate_up, other_gate_up = columns(core), swap(columns(1 - core), "c")
    gain = norm_gain[None, :]
    inverse = 1.0 / (gain * gain)
    other_inverse = swap(inverse, "c")

    heads = exchange(heads, "x").reshape(NX * tokens, SLICE)
    picks = spread(slots, jnp.ones_like(slots))
    heads, gate_up, other_gate_up, inverse, other_inverse, picks = lax.optimization_barrier(
        (heads, gate_up, other_gate_up, inverse, other_inverse, picks)
    )
    other_heads = swap(heads, "c")
    partial = jnp.dot(
        heads,
        lax.dynamic_slice_in_dim(quarter, core * SLICE, SLICE, 0),
        preferred_element_type=f32,
    ) + jnp.dot(
        other_heads,
        lax.dynamic_slice_in_dim(quarter, (1 - core) * SLICE, SLICE, 0),
        preferred_element_type=f32,
    )
    terms = exchange(partial.astype(bf16).reshape(NX, tokens, SLICE), "x")
    stream = residual.astype(f32) + jnp.sum(terms.astype(f32), axis=0)

    scaled = (stream * gain).astype(bf16)
    outgoing = jnp.dot(picks, scaled, preferred_element_type=f32).astype(bf16)
    incoming = exchange(outgoing.reshape(N_CTX, GROUP, SLICE), CTX).reshape(SENT, SLICE)
    part, squares = products(
        incoming, swap(incoming, "c"), gate_up, other_gate_up, inverse, other_inverse
    )
    squares, slots, route_gates, w_down, stream = lax.optimization_barrier(
        (squares, slots, route_gates, w_down, stream)
    )
    stream_out = stream.astype(bf16)
    combine = spread(slots, route_gates.astype(f32).T)
    down = lax.dynamic_slice_in_dim(w_down[0], core * half, half, 0)
    other_down = lax.dynamic_slice_in_dim(w_down[0], (1 - core) * half, half, 0)
    totals = lax.psum(squares[:, 0], "h")
    total = lax.dynamic_index_in_dim(totals, lax.axis_index("h"), 0, keepdims=False)[:SHARE]
    scale = lax.rsqrt(total / D + epsilon)[:, None]
    sums = lax.psum_scatter(part.reshape(ROWS, FF), "h", scatter_dimension=0, tiled=True)
    sums, scale, combine, down, other_down, stream_out = lax.optimization_barrier(
        (sums, scale, combine, down, other_down, stream_out)
    )
    sums = sums.astype(f32) * scale
    hidden = (jax.nn.silu(sums[:, :half]) * sums[:, half:]).astype(bf16)
    all_hidden = lax.all_gather(hidden, "h", axis=0, tiled=True)
    results = expert_results(all_hidden, swap(all_hidden, "c"), down, other_down)
    returned = exchange(results.reshape(N_CTX, GROUP, SLICE), CTX).reshape(SENT, SLICE)
    expert_out = jnp.einsum("rt,rd->td", combine, returned, preferred_element_type=f32)
    return stream_out, expert_out.astype(bf16)


def solution(mesh):
    split = Mesh(np.asarray(mesh.devices).reshape(NX, NY, NL, NH, NC), ("x", "y", "l", "h", "c"))
    ctx, exp = CTX, ("h", "c")
    placed = (
        P(ctx, exp),
        P(ctx, None),
        P(ctx, None),
        P(ctx, exp),
        P(ctx, exp),
        P(exp),
        P(ctx, exp, None),
        P(ctx, exp, None),
        P(ctx, None, exp),
        P(ctx, None),
        P(ctx, None),
        P(ctx, None),
        P(ctx, None),
        P(ctx),
    )
    return jax.shard_map(
        body,
        mesh=split,
        in_specs=placed,
        out_specs=(P(ctx, exp), P(ctx, exp)),
        check_vma=False,
    )
```

```python
import jax
import jax.numpy as jnp
import numpy as np
from jax import lax
from jax.experimental import pallas as pl
from jax.experimental.pallas import tpu as pltpu
from jax.sharding import Mesh, PartitionSpec as P

D = 4096
HD = 128
TOPK = 8
QH = 32
KVH = 2
FF = 768
FIX = 32
TOK = 128
SLOTS = 21
GROUP = 24
NX, NY, NL, NH, NC = 4, 8, 2, 4, 2
N_CTX = NX * NY * NL
GRID = NX * NY
SENT = GRID * GROUP
ROWS = GRID * SLOTS
SHARE = ROWS // NH
LANES = 256
EXTRA = 8
PACK = 8 * SLOTS
PACK_SENT = 8 * GROUP
SLICE = D // (NH * NC)
CTX = ("x", "y", "l")
f32, bf16 = jnp.float32, jnp.bfloat16

epsilon = 1e-06


def swap(block, axis):
    return lax.ppermute(block, axis, [(0, 1), (1, 0)])


def exchange(blocks, axes):
    return lax.all_to_all(blocks, axes, split_axis=0, concat_axis=0, tiled=True)


def from_behind(block, distance):
    route = [(i, i + distance) for i in range(N_CTX - distance)]
    return lax.ppermute(block, CTX, route)


def attention(queries, key_rows, value_rows):
    tokens = queries.shape[0]
    block = lax.axis_index(CTX)
    kv_first = lax.axis_index("h") // 2 * HD
    own = jnp.concatenate(
        [
            lax.dynamic_slice_in_dim(key_rows, kv_first, HD, 1),
            lax.dynamic_slice_in_dim(value_rows, kv_first, HD, 1),
        ],
        axis=1,
    )
    pairs = [from_behind(own, 3), from_behind(own, 2), from_behind(own, 1), own]
    keys = jnp.concatenate([pair[:, :HD] for pair in pairs], axis=0)
    values = jnp.concatenate([pair[:, HD:] for pair in pairs], axis=0)
    q_view = queries.reshape(tokens, -1, HD)
    scores = jnp.einsum("tgd,sd->gts", q_view, keys, preferred_element_type=f32) / HD**0.5
    q_pos = block * tokens + jnp.arange(tokens)
    k_pos = (block - 3) * tokens + jnp.arange(4 * tokens)
    allowed = (k_pos[None, :] >= 0) & (k_pos[None, :] <= q_pos[:, None])
    scores = jnp.where(allowed, scores, -1e30)
    highest = jnp.max(scores, axis=2, keepdims=True)
    weights = jnp.where(allowed, jnp.exp(scores - highest), 0.0)
    denominators = jnp.sum(weights, axis=2, keepdims=True)
    mixed = (
        jnp.einsum("gts,sd->gtd", weights.astype(bf16), values, preferred_element_type=f32)
        / denominators
    )
    return jnp.transpose(mixed, (1, 0, 2)).reshape(tokens, -1).astype(bf16)


def slots_of(pred_ids, fix_pair, fix_expert, fix_count):
    tokens = pred_ids.shape[0]
    places = jnp.arange(tokens * TOPK, dtype=jnp.int32).reshape(tokens, TOPK)
    live = jnp.arange(FIX) < fix_count[0]
    hit = (places[:, :, None] == fix_pair[0][None, None, :]) & live[None, None, :]
    fixed = jnp.sum(jnp.where(hit, fix_expert[0][None, None, :], 0), axis=2)
    ids = jnp.where(jnp.any(hit, axis=2), fixed, pred_ids)
    named = ids[:, :, None] == jnp.arange(N_CTX)[None, None, :]
    counts = jnp.sum(named.astype(f32), axis=1)
    earlier = (
        jnp.arange(tokens)[:, None] > jnp.arange(tokens)[None, :]
    ).astype(bf16)
    before = jnp.dot(earlier, counts.astype(bf16), preferred_element_type=f32)
    rank = jnp.sum(jnp.where(named, before[:, None, :], 0.0), axis=2)
    twin = (ids[:, :, None] == ids[:, None, :]) & (
        jnp.arange(TOPK)[None, :, None] > jnp.arange(TOPK)[None, None, :]
    )
    rank = rank + jnp.sum(twin.astype(f32), axis=2)
    return ids.astype(f32), rank


def row_slots(table, side):
    ids, rank, gates = table[:TOPK], table[TOPK : 2 * TOPK], table[2 * TOPK :]
    column = jnp.floor(ids * 0.5)
    return jnp.where(ids - 2.0 * column == side, column * GROUP + rank, -1.0), gates


def spread(slots, values):
    row_ids = jnp.arange(SENT, dtype=f32)[:, None]
    total = jnp.zeros((SENT, slots.shape[1]), f32)
    for k in range(TOPK):
        total = total + jnp.where(slots[k][None, :] == row_ids, values[k][None, :], 0.0)
    return total.astype(bf16)


def packing():
    place = np.arange(PACK)
    return (place // SLOTS * GROUP + place % SLOTS)[:, None] == np.arange(PACK_SENT)[None, :]


def products_kernel(
    own_ref, other_ref, w_own_ref, w_other_ref, inv_own_ref, inv_other_ref, pick_ref, part_ref
):
    pick = pick_ref[...]
    ones = jnp.ones((8, SLICE), bf16)
    blank = jnp.zeros((LANES - SHARE, SLICE), bf16)
    row = lax.broadcasted_iota(jnp.int32, (EXTRA, FF), 0)

    def squares(rows, inverse_ref):
        weighted = (rows * rows * inverse_ref[...]).astype(bf16)
        return lax.dot_general(
            ones,
            jnp.concatenate([weighted, blank], axis=0),
            (((1,), (1,)), ((), ())),
            preferred_element_type=f32,
        )

    for h in range(NH):
        taken = slice(h * PACK_SENT, (h + 1) * PACK_SENT)
        own = jnp.dot(pick, own_ref[taken], preferred_element_type=f32)
        other = jnp.dot(pick, other_ref[taken], preferred_element_type=f32)
        part = jnp.dot(own.astype(bf16), w_own_ref[...], preferred_element_type=f32) + jnp.dot(
            other.astype(bf16), w_other_ref[...], preferred_element_type=f32
        )
        total = squares(own, inv_own_ref) + squares(other, inv_other_ref)
        total = jnp.concatenate([total, jnp.zeros((8, FF - LANES), f32)], axis=1)
        high = total.astype(bf16).astype(f32)
        tail = jnp.where(row == 0, high, jnp.where(row == 1, total - high, 0.0))
        part_ref[h] = jnp.concatenate([part, tail], axis=0).astype(bf16)


def products(own, other, w_own, w_other, inv_own, inv_other):
    return pl.pallas_call(
        products_kernel,
        out_shape=jax.ShapeDtypeStruct((NH, SHARE + EXTRA, FF), bf16),
        compiler_params=pltpu.CompilerParams(vmem_limit_bytes=48 * 1024 * 1024),
        cost_estimate=pl.CostEstimate(flops=100_000_000, bytes_accessed=500_000, transcendentals=0),
    )(own, other, w_own, w_other, inv_own, inv_other, jnp.asarray(packing(), bf16))


def results_kernel(own_ref, other_ref, down_own_ref, down_other_ref, place_ref, out_ref):
    place = place_ref[...]
    for i in range(NH // 2):
        rows = slice(2 * i * SHARE, 2 * (i + 1) * SHARE)
        part = jnp.dot(own_ref[rows], down_own_ref[...], preferred_element_type=f32) + jnp.dot(
            other_ref[rows], down_other_ref[...], preferred_element_type=f32
        )
        for j in range(2):
            rows = part[j * PACK : (j + 1) * PACK].astype(bf16)
            start = (2 * i + j) * PACK_SENT
            out_ref[start : start + PACK_SENT] = jnp.dot(
                place, rows, preferred_element_type=f32
            ).astype(bf16)


def expert_results(own, other, down_own, down_other):
    return pl.pallas_call(
        results_kernel,
        out_shape=jax.ShapeDtypeStruct((SENT, SLICE), bf16),
        compiler_params=pltpu.CompilerParams(vmem_limit_bytes=48 * 1024 * 1024),
        cost_estimate=pl.CostEstimate(flops=100_000_000, bytes_accessed=500_000, transcendentals=0),
    )(own, other, down_own, down_other, jnp.asarray(packing().T, bf16))


def body(
    queries,
    key_rows,
    value_rows,
    out_weight,
    residual,
    norm_gain,
    w_gate,
    w_up,
    w_down,
    pred_ids,
    route_gates,
    fix_pair,
    fix_expert,
    fix_count,
):
    core, side = lax.axis_index("c"), lax.axis_index("l")
    tokens = queries.shape[0]
    half = FF // 2

    other_strip = swap(out_weight, "l")
    strips = jnp.concatenate(
        [
            jnp.where(side == 0, out_weight, other_strip),
            jnp.where(side == 0, other_strip, out_weight),
        ],
        axis=0,
    )
    strips, queries = lax.optimization_barrier((strips, queries))
    quarter = lax.all_gather(strips, "y", axis=0, tiled=True)

    attended = attention(queries, key_rows, value_rows)
    heads = lax.all_gather(attended, "h", axis=0, tiled=True).reshape(NH, tokens, SLICE)
    heads = exchange(heads, "x").reshape(NX * tokens, SLICE)
    other_heads = swap(heads, "c")
    partial = jnp.dot(
        heads,
        lax.dynamic_slice_in_dim(quarter, core * SLICE, SLICE, 0),
        preferred_element_type=f32,
    ) + jnp.dot(
        other_heads,
        lax.dynamic_slice_in_dim(quarter, (1 - core) * SLICE, SLICE, 0),
        preferred_element_type=f32,
    )
    partial, pred_ids, fix_pair, w_gate, w_up, norm_gain = lax.optimization_barrier(
        (partial.astype(bf16), pred_ids, fix_pair, w_gate, w_up, norm_gain)
    )

    ids, rank = slots_of(pred_ids, fix_pair, fix_expert, fix_count)
    table = jnp.concatenate([ids, rank, route_gates.astype(f32)], axis=1)
    slots, gates = row_slots(table.T, side.astype(f32))
    pick = spread(slots, jnp.ones_like(slots))

    def columns(which):
        return jnp.concatenate(
            [
                lax.dynamic_slice_in_dim(w_gate[0], which * half, half, 1),
                lax.dynamic_slice_in_dim(w_up[0], which * half, half, 1),
            ],
            axis=1,
        )

    gate_up, other_gate_up = columns(core), swap(columns(1 - core), "c")
    down = lax.dynamic_slice_in_dim(w_down[0], core * half, half, 0)
    other_down = lax.dynamic_slice_in_dim(w_down[0], (1 - core) * half, half, 0)
    gain = norm_gain[None, :]
    inverse = 1.0 / (gain * gain)
    other_inverse = swap(inverse, "c")

    terms = exchange(partial.reshape(NX, tokens, SLICE), "x")
    other_slots, other_gates = row_slots(swap(table, "l").T, side.astype(f32))
    other_pick = spread(other_slots, jnp.ones_like(other_slots))
    terms, pick = lax.optimization_barrier((terms, pick))
    stream = residual.astype(f32) + jnp.sum(terms.astype(f32), axis=0)

    scaled = (stream * gain).astype(bf16)
    beside = swap(scaled, "l")

    def through(rows):
        return exchange(rows.reshape(GRID, GROUP, SLICE), ("x", "y")).reshape(SENT, SLICE)

    def sent(pick, rows):
        return through(jnp.dot(pick, rows, preferred_element_type=f32).astype(bf16))

    def share_products(rows):
        return products(rows, swap(rows, "c"), gate_up, other_gate_up, inverse, other_inverse)

    def reduced(part):
        flat = part.reshape(NH * (SHARE + EXTRA), FF)
        return lax.psum_scatter(flat, "h", scatter_dimension=0, tiled=True)

    def gathered(sums):
        sums = sums.astype(f32)
        total = (sums[SHARE] + sums[SHARE + 1])[:SHARE]
        sums = sums[:SHARE] * lax.rsqrt(total / D + epsilon)[:, None]
        hidden = (jax.nn.silu(sums[:, :half]) * sums[:, half:]).astype(bf16)
        return lax.all_gather(hidden, "h", axis=0, tiled=True)

    def finished(hidden):
        return expert_results(hidden, swap(hidden, "c"), down, other_down)

    first = sent(pick, scaled)
    first, beside, other_pick, gate_up, other_gate_up, inverse, other_inverse = (
        lax.optimization_barrier(
            (first, beside, other_pick, gate_up, other_gate_up, inverse, other_inverse)
        )
    )
    first = share_products(first)
    first, beside = lax.optimization_barrier((first, beside))
    second = share_products(sent(other_pick, beside))
    first, second = reduced(first), reduced(second)
    first = through(finished(gathered(first)))
    hidden = gathered(second)
    combine = spread(other_slots, other_gates)
    first, hidden, combine = lax.optimization_barrier((first, hidden, combine))
    second = through(finished(hidden))
    mixed = jnp.einsum("rt,rd->td", spread(slots, gates), first, preferred_element_type=f32)
    other_mixed = jnp.einsum("rt,rd->td", combine, second, preferred_element_type=f32)
    expert_out = mixed + swap(other_mixed.astype(bf16), "l").astype(f32)
    return stream.astype(bf16), expert_out.astype(bf16)


def solution(mesh):
    split = Mesh(np.asarray(mesh.devices).reshape(NX, NY, NL, NH, NC), ("x", "y", "l", "h", "c"))
    ctx, exp = CTX, ("h", "c")
    placed = (
        P(ctx, exp),
        P(ctx, None),
        P(ctx, None),
        P(ctx, exp),
        P(ctx, exp),
        P(exp),
        P(ctx, exp, None),
        P(ctx, exp, None),
        P(ctx, None, exp),
        P(ctx, None),
        P(ctx, None),
        P(ctx, None),
        P(ctx, None),
        P(ctx),
    )
    return jax.shard_map(
        body,
        mesh=split,
        in_specs=placed,
        out_specs=(P(ctx, exp), P(ctx, exp)),
        check_vma=False,
    )
```

```python
import jax
import jax.numpy as jnp
import numpy as np
from jax import lax
from jax.experimental import pallas as pl
from jax.experimental.pallas import tpu as pltpu
from jax.sharding import Mesh, PartitionSpec as P

D = 4096
HD = 128
TOPK = 8
QH = 32
KVH = 2
FF = 768
FIX = 32
TOK = 128
SLOTS = 21
GROUP = 24
NX, NY, NL, NH, NC = 4, 8, 2, 4, 2
N_CTX = NX * NY * NL
GRID = NX * NY
SENT = GRID * GROUP
ROWS = GRID * SLOTS
SHARE = ROWS // NH
LANES = 256
EXTRA = 8
PACK = 8 * SLOTS
PACK_SENT = 8 * GROUP
SLICE = D // (NH * NC)
CTX = ("x", "y", "l")
f32, bf16 = jnp.float32, jnp.bfloat16

epsilon = 1e-06


def swap(block, axis):
    return lax.ppermute(block, axis, [(0, 1), (1, 0)])


def exchange(blocks, axes):
    return lax.all_to_all(blocks, axes, split_axis=0, concat_axis=0, tiled=True)


def from_behind(block, distance):
    route = [(i, i + distance) for i in range(N_CTX - distance)]
    return lax.ppermute(block, CTX, route)


def attention(queries, key_rows, value_rows):
    tokens = queries.shape[0]
    block = lax.axis_index(CTX)
    kv_first = lax.axis_index("h") // 2 * HD
    own = jnp.concatenate(
        [
            lax.dynamic_slice_in_dim(key_rows, kv_first, HD, 1),
            lax.dynamic_slice_in_dim(value_rows, kv_first, HD, 1),
        ],
        axis=1,
    )
    pairs = [from_behind(own, 3), from_behind(own, 2), from_behind(own, 1), own]
    keys = jnp.concatenate([pair[:, :HD] for pair in pairs], axis=0)
    values = jnp.concatenate([pair[:, HD:] for pair in pairs], axis=0)
    q_view = queries.reshape(tokens, -1, HD)
    scores = jnp.einsum("tgd,sd->gts", q_view, keys, preferred_element_type=f32) / HD**0.5
    q_pos = block * tokens + jnp.arange(tokens)
    k_pos = (block - 3) * tokens + jnp.arange(4 * tokens)
    allowed = (k_pos[None, :] >= 0) & (k_pos[None, :] <= q_pos[:, None])
    scores = jnp.where(allowed, scores, -1e30)
    highest = jnp.max(scores, axis=2, keepdims=True)
    weights = jnp.where(allowed, jnp.exp(scores - highest), 0.0)
    denominators = jnp.sum(weights, axis=2, keepdims=True)
    mixed = (
        jnp.einsum("gts,sd->gtd", weights.astype(bf16), values, preferred_element_type=f32)
        / denominators
    )
    return jnp.transpose(mixed, (1, 0, 2)).reshape(tokens, -1).astype(bf16)


def slots_of(pred_ids, fix_pair, fix_expert, fix_count):
    tokens = pred_ids.shape[0]
    places = jnp.arange(tokens * TOPK, dtype=jnp.int32).reshape(tokens, TOPK)
    live = jnp.arange(FIX) < fix_count[0]
    hit = (places[:, :, None] == fix_pair[0][None, None, :]) & live[None, None, :]
    fixed = jnp.sum(jnp.where(hit, fix_expert[0][None, None, :], 0), axis=2)
    ids = jnp.where(jnp.any(hit, axis=2), fixed, pred_ids)
    named = ids[:, :, None] == jnp.arange(N_CTX)[None, None, :]
    counts = jnp.sum(named.astype(f32), axis=1)
    earlier = (
        jnp.arange(tokens)[:, None] > jnp.arange(tokens)[None, :]
    ).astype(bf16)
    before = jnp.dot(earlier, counts.astype(bf16), preferred_element_type=f32)
    rank = jnp.sum(jnp.where(named, before[:, None, :], 0.0), axis=2)
    twin = (ids[:, :, None] == ids[:, None, :]) & (
        jnp.arange(TOPK)[None, :, None] > jnp.arange(TOPK)[None, None, :]
    )
    rank = rank + jnp.sum(twin.astype(f32), axis=2)
    return ids.astype(f32), rank


def row_slots(table, side):
    ids, rank, gates = table[:TOPK], table[TOPK : 2 * TOPK], table[2 * TOPK :]
    column = jnp.floor(ids * 0.5)
    return jnp.where(ids - 2.0 * column == side, column * GROUP + rank, -1.0), gates


def spread(slots, values):
    row_ids = jnp.arange(SENT, dtype=f32)[:, None]
    total = jnp.zeros((SENT, slots.shape[1]), f32)
    for k in range(TOPK):
        total = total + jnp.where(slots[k][None, :] == row_ids, values[k][None, :], 0.0)
    return total.astype(bf16)


def packing():
    place = np.arange(PACK)
    return (place // SLOTS * GROUP + place % SLOTS)[:, None] == np.arange(PACK_SENT)[None, :]


def products_kernel(
    own_ref, other_ref, w_own_ref, w_other_ref, inv_own_ref, inv_other_ref, pick_ref, part_ref
):
    pick = pick_ref[...]
    ones = jnp.ones((8, SLICE), bf16)
    blank = jnp.zeros((LANES - SHARE, SLICE), bf16)
    row = lax.broadcasted_iota(jnp.int32, (EXTRA, FF), 0)

    def squares(rows, inverse_ref):
        weighted = (rows * rows * inverse_ref[...]).astype(bf16)
        return lax.dot_general(
            ones,
            jnp.concatenate([weighted, blank], axis=0),
            (((1,), (1,)), ((), ())),
            preferred_element_type=f32,
        )

    for h in range(NH):
        taken = slice(h * PACK_SENT, (h + 1) * PACK_SENT)
        own = jnp.dot(pick, own_ref[taken], preferred_element_type=f32)
        other = jnp.dot(pick, other_ref[taken], preferred_element_type=f32)
        part = jnp.dot(own.astype(bf16), w_own_ref[...], preferred_element_type=f32) + jnp.dot(
            other.astype(bf16), w_other_ref[...], preferred_element_type=f32
        )
        total = squares(own, inv_own_ref) + squares(other, inv_other_ref)
        total = jnp.concatenate([total, jnp.zeros((8, FF - LANES), f32)], axis=1)
        high = total.astype(bf16).astype(f32)
        tail = jnp.where(row == 0, high, jnp.where(row == 1, total - high, 0.0))
        part_ref[h] = jnp.concatenate([part, tail], axis=0).astype(bf16)


def products(own, other, w_own, w_other, inv_own, inv_other):
    return pl.pallas_call(
        products_kernel,
        out_shape=jax.ShapeDtypeStruct((NH, SHARE + EXTRA, FF), bf16),
        compiler_params=pltpu.CompilerParams(vmem_limit_bytes=48 * 1024 * 1024),
        cost_estimate=pl.CostEstimate(flops=100_000_000, bytes_accessed=500_000, transcendentals=0),
    )(own, other, w_own, w_other, inv_own, inv_other, jnp.asarray(packing(), bf16))


def results_kernel(own_ref, other_ref, down_own_ref, down_other_ref, place_ref, out_ref):
    place = place_ref[...]
    for i in range(NH // 2):
        rows = slice(2 * i * SHARE, 2 * (i + 1) * SHARE)
        part = jnp.dot(own_ref[rows], down_own_ref[...], preferred_element_type=f32) + jnp.dot(
            other_ref[rows], down_other_ref[...], preferred_element_type=f32
        )
        for j in range(2):
            rows = part[j * PACK : (j + 1) * PACK].astype(bf16)
            start = (2 * i + j) * PACK_SENT
            out_ref[start : start + PACK_SENT] = jnp.dot(
                place, rows, preferred_element_type=f32
            ).astype(bf16)


def expert_results(own, other, down_own, down_other):
    return pl.pallas_call(
        results_kernel,
        out_shape=jax.ShapeDtypeStruct((SENT, SLICE), bf16),
        compiler_params=pltpu.CompilerParams(vmem_limit_bytes=48 * 1024 * 1024),
        cost_estimate=pl.CostEstimate(flops=100_000_000, bytes_accessed=500_000, transcendentals=0),
    )(own, other, down_own, down_other, jnp.asarray(packing().T, bf16))


def body(
    queries,
    key_rows,
    value_rows,
    out_weight,
    residual,
    norm_gain,
    w_gate,
    w_up,
    w_down,
    pred_ids,
    route_gates,
    fix_pair,
    fix_expert,
    fix_count,
):
    core, side = lax.axis_index("c"), lax.axis_index("l")
    tokens = queries.shape[0]
    half = FF // 2

    other_strip = swap(out_weight, "l")
    strips = jnp.concatenate(
        [
            jnp.where(side == 0, out_weight, other_strip),
            jnp.where(side == 0, other_strip, out_weight),
        ],
        axis=0,
    )
    strips, queries = lax.optimization_barrier((strips, queries))
    quarter = lax.all_gather(strips, "y", axis=0, tiled=True)

    attended = attention(queries, key_rows, value_rows)
    heads = lax.all_gather(attended, "h", axis=0, tiled=True).reshape(NH, tokens, SLICE)
    heads = exchange(heads, "x").reshape(NX * tokens, SLICE)
    other_heads = swap(heads, "c")
    partial = jnp.dot(
        heads,
        lax.dynamic_slice_in_dim(quarter, core * SLICE, SLICE, 0),
        preferred_element_type=f32,
    ) + jnp.dot(
        other_heads,
        lax.dynamic_slice_in_dim(quarter, (1 - core) * SLICE, SLICE, 0),
        preferred_element_type=f32,
    )
    partial, pred_ids, fix_pair, w_gate, w_up, norm_gain = lax.optimization_barrier(
        (partial.astype(bf16), pred_ids, fix_pair, w_gate, w_up, norm_gain)
    )

    ids, rank = slots_of(pred_ids, fix_pair, fix_expert, fix_count)
    table = jnp.concatenate([ids, rank, route_gates.astype(f32)], axis=1)
    slots, gates = row_slots(table.T, side.astype(f32))
    pick = spread(slots, jnp.ones_like(slots))

    def columns(which):
        return jnp.concatenate(
            [
                lax.dynamic_slice_in_dim(w_gate[0], which * half, half, 1),
                lax.dynamic_slice_in_dim(w_up[0], which * half, half, 1),
            ],
            axis=1,
        )

    gate_up, other_gate_up = columns(core), swap(columns(1 - core), "c")
    down = lax.dynamic_slice_in_dim(w_down[0], core * half, half, 0)
    other_down = lax.dynamic_slice_in_dim(w_down[0], (1 - core) * half, half, 0)
    gain = norm_gain[None, :]
    inverse = 1.0 / (gain * gain)
    other_inverse = swap(inverse, "c")

    terms = exchange(partial.reshape(NX, tokens, SLICE), "x")
    other_slots, other_gates = row_slots(swap(table, "l").T, side.astype(f32))
    other_pick = spread(other_slots, jnp.ones_like(other_slots))
    terms, pick = lax.optimization_barrier((terms, pick))
    stream = residual.astype(f32) + jnp.sum(terms.astype(f32), axis=0)

    scaled = (stream * gain).astype(bf16)
    beside = swap(scaled, "l")

    def through(rows):
        return exchange(rows.reshape(GRID, GROUP, SLICE), ("x", "y")).reshape(SENT, SLICE)

    def sent(pick, rows):
        return through(jnp.dot(pick, rows, preferred_element_type=f32).astype(bf16))

    def share_products(rows):
        return products(rows, swap(rows, "c"), gate_up, other_gate_up, inverse, other_inverse)

    def reduced(part):
        flat = part.reshape(NH * (SHARE + EXTRA), FF)
        return lax.psum_scatter(flat, "h", scatter_dimension=0, tiled=True).astype(f32)

    def gathered(sums):
        total = (sums[SHARE] + sums[SHARE + 1])[:SHARE]
        sums = sums[:SHARE] * lax.rsqrt(total / D + epsilon)[:, None]
        hidden = (jax.nn.silu(sums[:, :half]) * sums[:, half:]).astype(bf16)
        return lax.all_gather(hidden, "h", axis=0, tiled=True)

    def finished(hidden):
        return expert_results(hidden, swap(hidden, "c"), down, other_down)

    first = sent(pick, scaled)
    first, beside, other_pick, gate_up, other_gate_up, inverse, other_inverse = (
        lax.optimization_barrier(
            (first, beside, other_pick, gate_up, other_gate_up, inverse, other_inverse)
        )
    )
    first = share_products(first)
    second = share_products(sent(other_pick, beside))
    first, parts = reduced(first), exchange(second, "h")
    first = through(finished(gathered(first)))
    hidden = gathered(jnp.sum(parts.astype(f32), axis=0))
    combine = spread(other_slots, other_gates)
    first, hidden, combine = lax.optimization_barrier((first, hidden, combine))
    second = through(finished(hidden))
    mixed = jnp.einsum("rt,rd->td", spread(slots, gates), first, preferred_element_type=f32)
    other_mixed = jnp.einsum("rt,rd->td", combine, second, preferred_element_type=f32)
    expert_out = mixed + swap(other_mixed.astype(bf16), "l").astype(f32)
    return stream.astype(bf16), expert_out.astype(bf16)


def solution(mesh):
    split = Mesh(np.asarray(mesh.devices).reshape(NX, NY, NL, NH, NC), ("x", "y", "l", "h", "c"))
    ctx, exp = CTX, ("h", "c")
    placed = (
        P(ctx, exp),
        P(ctx, None),
        P(ctx, None),
        P(ctx, exp),
        P(ctx, exp),
        P(exp),
        P(ctx, exp, None),
        P(ctx, exp, None),
        P(ctx, None, exp),
        P(ctx, None),
        P(ctx, None),
        P(ctx, None),
        P(ctx, None),
        P(ctx),
    )
    return jax.shard_map(
        body,
        mesh=split,
        in_specs=placed,
        out_specs=(P(ctx, exp), P(ctx, exp)),
        check_vma=False,
    )
```

```python
import jax
import jax.numpy as jnp
import numpy as np
from jax import lax
from jax.experimental import pallas as pl
from jax.experimental.pallas import tpu as pltpu
from jax.sharding import Mesh, PartitionSpec as P

D = 4096
HD = 128
TOPK = 8
QH = 32
KVH = 2
FF = 768
FIX = 32
TOK = 128
SLOTS = 21
GROUP = 24
NX, NY, NL, NH, NC = 4, 8, 2, 4, 2
N_CTX = NX * NY * NL
GRID = NX * NY
SENT = GRID * GROUP
ROWS = GRID * SLOTS
SHARE = ROWS // NH
LANES = 256
EXTRA = 8
PACK = 8 * SLOTS
PACK_SENT = 8 * GROUP
SLICE = D // (NH * NC)
CTX = ("x", "y", "l")
f32, bf16 = jnp.float32, jnp.bfloat16

epsilon = 1e-06


def swap(block, axis):
    return lax.ppermute(block, axis, [(0, 1), (1, 0)])


def exchange(blocks, axes):
    return lax.all_to_all(blocks, axes, split_axis=0, concat_axis=0, tiled=True)


def from_behind(block, distance):
    route = [(i, i + distance) for i in range(N_CTX - distance)]
    return lax.ppermute(block, CTX, route)


def attention(queries, key_rows, value_rows):
    tokens = queries.shape[0]
    block = lax.axis_index(CTX)
    kv_first = lax.axis_index("h") // 2 * HD
    own = jnp.concatenate(
        [
            lax.dynamic_slice_in_dim(key_rows, kv_first, HD, 1),
            lax.dynamic_slice_in_dim(value_rows, kv_first, HD, 1),
        ],
        axis=1,
    )
    pairs = [from_behind(own, 3), from_behind(own, 2), from_behind(own, 1), own]
    keys = jnp.concatenate([pair[:, :HD] for pair in pairs], axis=0)
    values = jnp.concatenate([pair[:, HD:] for pair in pairs], axis=0)
    q_view = queries.reshape(tokens, -1, HD)
    scores = jnp.einsum("tgd,sd->gts", q_view, keys, preferred_element_type=f32) / HD**0.5
    q_pos = block * tokens + jnp.arange(tokens)
    k_pos = (block - 3) * tokens + jnp.arange(4 * tokens)
    allowed = (k_pos[None, :] >= 0) & (k_pos[None, :] <= q_pos[:, None])
    scores = jnp.where(allowed, scores, -1e30)
    highest = jnp.max(scores, axis=2, keepdims=True)
    weights = jnp.where(allowed, jnp.exp(scores - highest), 0.0)
    denominators = jnp.sum(weights, axis=2, keepdims=True)
    mixed = (
        jnp.einsum("gts,sd->gtd", weights.astype(bf16), values, preferred_element_type=f32)
        / denominators
    )
    return jnp.transpose(mixed, (1, 0, 2)).reshape(tokens, -1).astype(bf16)


def slots_of(pred_ids, fix_pair, fix_expert, fix_count):
    tokens = pred_ids.shape[0]
    places = jnp.arange(tokens * TOPK, dtype=jnp.int32).reshape(tokens, TOPK)
    live = jnp.arange(FIX) < fix_count[0]
    hit = (places[:, :, None] == fix_pair[0][None, None, :]) & live[None, None, :]
    fixed = jnp.sum(jnp.where(hit, fix_expert[0][None, None, :], 0), axis=2)
    ids = jnp.where(jnp.any(hit, axis=2), fixed, pred_ids)
    named = ids[:, :, None] == jnp.arange(N_CTX)[None, None, :]
    counts = jnp.sum(named.astype(f32), axis=1)
    earlier = (
        jnp.arange(tokens)[:, None] > jnp.arange(tokens)[None, :]
    ).astype(bf16)
    before = jnp.dot(earlier, counts.astype(bf16), preferred_element_type=f32)
    rank = jnp.sum(jnp.where(named, before[:, None, :], 0.0), axis=2)
    twin = (ids[:, :, None] == ids[:, None, :]) & (
        jnp.arange(TOPK)[None, :, None] > jnp.arange(TOPK)[None, None, :]
    )
    rank = rank + jnp.sum(twin.astype(f32), axis=2)
    return ids.astype(f32), rank


def row_slots(table, side):
    ids, rank, gates = table[:TOPK], table[TOPK : 2 * TOPK], table[2 * TOPK :]
    column = jnp.floor(ids * 0.5)
    return jnp.where(ids - 2.0 * column == side, column * GROUP + rank, -1.0), gates


def spread(slots, values):
    row_ids = jnp.arange(SENT, dtype=f32)[:, None]
    total = jnp.zeros((SENT, slots.shape[1]), f32)
    for k in range(TOPK):
        total = total + jnp.where(slots[k][None, :] == row_ids, values[k][None, :], 0.0)
    return total.astype(bf16)


def packing():
    place = np.arange(PACK)
    return (place // SLOTS * GROUP + place % SLOTS)[:, None] == np.arange(PACK_SENT)[None, :]


def products_kernel(
    own_ref, other_ref, w_own_ref, w_other_ref, inv_own_ref, inv_other_ref, pick_ref, part_ref
):
    pick = pick_ref[...]
    ones = jnp.ones((8, SLICE), bf16)
    blank = jnp.zeros((LANES - SHARE, SLICE), bf16)
    row = lax.broadcasted_iota(jnp.int32, (EXTRA, FF), 0)

    def squares(rows, inverse_ref):
        weighted = (rows * rows * inverse_ref[...]).astype(bf16)
        return lax.dot_general(
            ones,
            jnp.concatenate([weighted, blank], axis=0),
            (((1,), (1,)), ((), ())),
            preferred_element_type=f32,
        )

    for h in range(NH):
        taken = slice(h * PACK_SENT, (h + 1) * PACK_SENT)
        own = jnp.dot(pick, own_ref[taken], preferred_element_type=f32)
        other = jnp.dot(pick, other_ref[taken], preferred_element_type=f32)
        part = jnp.dot(own.astype(bf16), w_own_ref[...], preferred_element_type=f32) + jnp.dot(
            other.astype(bf16), w_other_ref[...], preferred_element_type=f32
        )
        total = squares(own, inv_own_ref) + squares(other, inv_other_ref)
        total = jnp.concatenate([total, jnp.zeros((8, FF - LANES), f32)], axis=1)
        high = total.astype(bf16).astype(f32)
        tail = jnp.where(row == 0, high, jnp.where(row == 1, total - high, 0.0))
        part_ref[h] = jnp.concatenate([part, tail], axis=0).astype(bf16)


def products(own, other, w_own, w_other, inv_own, inv_other):
    return pl.pallas_call(
        products_kernel,
        out_shape=jax.ShapeDtypeStruct((NH, SHARE + EXTRA, FF), bf16),
        compiler_params=pltpu.CompilerParams(vmem_limit_bytes=48 * 1024 * 1024),
        cost_estimate=pl.CostEstimate(flops=100_000_000, bytes_accessed=500_000, transcendentals=0),
    )(own, other, w_own, w_other, inv_own, inv_other, jnp.asarray(packing(), bf16))


def results_kernel(own_ref, other_ref, down_own_ref, down_other_ref, place_ref, out_ref):
    place = place_ref[...]
    for i in range(NH // 2):
        rows = slice(2 * i * SHARE, 2 * (i + 1) * SHARE)
        part = jnp.dot(own_ref[rows], down_own_ref[...], preferred_element_type=f32) + jnp.dot(
            other_ref[rows], down_other_ref[...], preferred_element_type=f32
        )
        for j in range(2):
            rows = part[j * PACK : (j + 1) * PACK].astype(bf16)
            start = (2 * i + j) * PACK_SENT
            out_ref[start : start + PACK_SENT] = jnp.dot(
                place, rows, preferred_element_type=f32
            ).astype(bf16)


def expert_results(own, other, down_own, down_other):
    return pl.pallas_call(
        results_kernel,
        out_shape=jax.ShapeDtypeStruct((SENT, SLICE), bf16),
        compiler_params=pltpu.CompilerParams(vmem_limit_bytes=48 * 1024 * 1024),
        cost_estimate=pl.CostEstimate(flops=100_000_000, bytes_accessed=500_000, transcendentals=0),
    )(own, other, down_own, down_other, jnp.asarray(packing().T, bf16))


def body(
    queries,
    key_rows,
    value_rows,
    out_weight,
    residual,
    norm_gain,
    w_gate,
    w_up,
    w_down,
    pred_ids,
    route_gates,
    fix_pair,
    fix_expert,
    fix_count,
):
    core, side = lax.axis_index("c"), lax.axis_index("l")
    tokens = queries.shape[0]
    half = FF // 2

    other_strip = swap(out_weight, "l")
    strips = jnp.where(
        side == 0,
        jnp.concatenate([out_weight, other_strip], axis=0),
        jnp.concatenate([other_strip, out_weight], axis=0),
    )
    strips, queries = lax.optimization_barrier((strips, queries))
    quarter = lax.all_gather(strips, "y", axis=0, tiled=True)

    attended = attention(queries, key_rows, value_rows)
    heads = exchange(jnp.broadcast_to(attended[None], (NH, *attended.shape)), "h")
    heads = exchange(heads, "x").reshape(NX * tokens, SLICE)
    other_heads = swap(heads, "c")
    partial = jnp.dot(
        heads,
        lax.dynamic_slice_in_dim(quarter, core * SLICE, SLICE, 0),
        preferred_element_type=f32,
    ) + jnp.dot(
        other_heads,
        lax.dynamic_slice_in_dim(quarter, (1 - core) * SLICE, SLICE, 0),
        preferred_element_type=f32,
    )
    partial, pred_ids, fix_pair, w_gate, w_up, norm_gain = lax.optimization_barrier(
        (partial.astype(bf16), pred_ids, fix_pair, w_gate, w_up, norm_gain)
    )

    ids, rank = slots_of(pred_ids, fix_pair, fix_expert, fix_count)
    table = jnp.concatenate([ids, rank, route_gates.astype(f32)], axis=1)
    slots, gates = row_slots(table.T, side.astype(f32))
    pick = spread(slots, jnp.ones_like(slots))

    def columns(which):
        return jnp.concatenate(
            [
                lax.dynamic_slice_in_dim(w_gate[0], which * half, half, 1),
                lax.dynamic_slice_in_dim(w_up[0], which * half, half, 1),
            ],
            axis=1,
        )

    gate_up, other_gate_up = columns(core), swap(columns(1 - core), "c")
    down = lax.dynamic_slice_in_dim(w_down[0], core * half, half, 0)
    other_down = lax.dynamic_slice_in_dim(w_down[0], (1 - core) * half, half, 0)
    gain = norm_gain[None, :]
    inverse = 1.0 / (gain * gain)
    other_inverse = swap(inverse, "c")

    terms = exchange(partial.reshape(NX, tokens, SLICE), "x")
    other_slots, other_gates = row_slots(swap(table, "l").T, side.astype(f32))
    other_pick = spread(other_slots, jnp.ones_like(other_slots))
    terms, pick = lax.optimization_barrier((terms, pick))
    stream = residual.astype(f32) + jnp.sum(terms.astype(f32), axis=0)

    scaled = (stream * gain).astype(bf16)
    beside = swap(scaled, "l")

    def through(rows):
        return exchange(rows.reshape(GRID, GROUP, SLICE), ("x", "y")).reshape(SENT, SLICE)

    def sent(pick, rows):
        return through(jnp.dot(pick, rows, preferred_element_type=f32).astype(bf16))

    def share_products(rows):
        return products(rows, swap(rows, "c"), gate_up, other_gate_up, inverse, other_inverse)

    def reduced(part):
        flat = part.reshape(NH * (SHARE + EXTRA), FF)
        return lax.psum_scatter(flat, "h", scatter_dimension=0, tiled=True)

    def gathered(sums):
        sums = sums.astype(f32)
        total = (sums[SHARE] + sums[SHARE + 1])[:SHARE]
        sums = sums[:SHARE] * lax.rsqrt(total / D + epsilon)[:, None]
        hidden = (jax.nn.silu(sums[:, :half]) * sums[:, half:]).astype(bf16)
        return lax.all_gather(hidden, "h", axis=0, tiled=True)

    def finished(hidden):
        return expert_results(hidden, swap(hidden, "c"), down, other_down)

    first = sent(pick, scaled)
    first, beside, other_pick, gate_up, other_gate_up, inverse, other_inverse = (
        lax.optimization_barrier(
            (first, beside, other_pick, gate_up, other_gate_up, inverse, other_inverse)
        )
    )
    first = reduced(share_products(first))
    second = sent(other_pick, beside)
    first, second = lax.optimization_barrier((first, second))
    second = reduced(share_products(second))
    first = through(finished(gathered(first)))
    hidden = gathered(second)
    combine = spread(other_slots, other_gates)
    first, hidden, combine = lax.optimization_barrier((first, hidden, combine))
    second = through(finished(hidden))
    mixed = jnp.einsum("rt,rd->td", spread(slots, gates), first, preferred_element_type=f32)
    other_mixed = jnp.einsum("rt,rd->td", combine, second, preferred_element_type=f32)
    expert_out = mixed + swap(other_mixed.astype(bf16), "l").astype(f32)
    return stream.astype(bf16), expert_out.astype(bf16)


def solution(mesh):
    split = Mesh(np.asarray(mesh.devices).reshape(NX, NY, NL, NH, NC), ("x", "y", "l", "h", "c"))
    ctx, exp = CTX, ("h", "c")
    placed = (
        P(ctx, exp),
        P(ctx, None),
        P(ctx, None),
        P(ctx, exp),
        P(ctx, exp),
        P(exp),
        P(ctx, exp, None),
        P(ctx, exp, None),
        P(ctx, None, exp),
        P(ctx, None),
        P(ctx, None),
        P(ctx, None),
        P(ctx, None),
        P(ctx),
    )
    return jax.shard_map(
        body,
        mesh=split,
        in_specs=placed,
        out_specs=(P(ctx, exp), P(ctx, exp)),
        check_vma=False,
    )
```

```python
import functools

import jax
import jax.numpy as jnp
import numpy as np
from jax import lax
from jax.experimental import pallas as pl
from jax.experimental.pallas import tpu as pltpu
from jax.sharding import Mesh, PartitionSpec as P

D = 4096
HD = 128
TOPK = 8
QH = 32
KVH = 2
FF = 768
FIX = 32
TOK = 128
NX, NY, NL, NH, NC = 4, 8, 2, 4, 2
N_CTX = NX * NY * NL
PEERS = 8
EXTRA = 8
PARTS = ((0, 8, 8), (8, 13, 16))
SLICE = D // (NH * NC)
CTX = ("x", "y", "l")
f32, bf16 = jnp.float32, jnp.bfloat16

epsilon = 1e-06


def swap(block, axis):
    return lax.ppermute(block, axis, [(0, 1), (1, 0)])


def exchange(blocks, axes):
    return lax.all_to_all(blocks, axes, split_axis=0, concat_axis=0, tiled=True)


def from_behind(block, distance):
    route = [(i, i + distance) for i in range(N_CTX - distance)]
    return lax.ppermute(block, CTX, route)


def attention(queries, key_rows, value_rows):
    tokens = queries.shape[0]
    block = lax.axis_index(CTX)
    kv_first = lax.axis_index("h") // 2 * HD
    own = jnp.concatenate(
        [
            lax.dynamic_slice_in_dim(key_rows, kv_first, HD, 1),
            lax.dynamic_slice_in_dim(value_rows, kv_first, HD, 1),
        ],
        axis=1,
    )
    pairs = [from_behind(own, 3), from_behind(own, 2), from_behind(own, 1), own]
    keys = jnp.concatenate([pair[:, :HD] for pair in pairs], axis=0)
    values = jnp.concatenate([pair[:, HD:] for pair in pairs], axis=0)
    q_view = queries.reshape(tokens, -1, HD)
    scores = jnp.einsum("tgd,sd->gts", q_view, keys, preferred_element_type=f32) / HD**0.5
    q_pos = block * tokens + jnp.arange(tokens)
    k_pos = (block - 3) * tokens + jnp.arange(4 * tokens)
    allowed = (k_pos[None, :] >= 0) & (k_pos[None, :] <= q_pos[:, None])
    scores = jnp.where(allowed, scores, -1e30)
    highest = jnp.max(scores, axis=2, keepdims=True)
    weights = jnp.where(allowed, jnp.exp(scores - highest), 0.0)
    denominators = jnp.sum(weights, axis=2, keepdims=True)
    mixed = (
        jnp.einsum("gts,sd->gtd", weights.astype(bf16), values, preferred_element_type=f32)
        / denominators
    )
    return jnp.transpose(mixed, (1, 0, 2)).reshape(tokens, -1).astype(bf16)


def slots_of(pred_ids, fix_pair, fix_expert, fix_count):
    tokens = pred_ids.shape[0]
    places = jnp.arange(tokens * TOPK, dtype=jnp.int32).reshape(tokens, TOPK)
    live = jnp.arange(FIX) < fix_count[0]
    hit = (places[:, :, None] == fix_pair[0][None, None, :]) & live[None, None, :]
    fixed = jnp.sum(jnp.where(hit, fix_expert[0][None, None, :], 0), axis=2)
    ids = jnp.where(jnp.any(hit, axis=2), fixed, pred_ids)
    named = ids[:, :, None] == jnp.arange(N_CTX)[None, None, :]
    counts = jnp.sum(named.astype(f32), axis=1)
    earlier = (
        jnp.arange(tokens)[:, None] > jnp.arange(tokens)[None, :]
    ).astype(bf16)
    before = jnp.dot(earlier, counts.astype(bf16), preferred_element_type=f32)
    rank = jnp.sum(jnp.where(named, before[:, None, :], 0.0), axis=2)
    twin = (ids[:, :, None] == ids[:, None, :]) & (
        jnp.arange(TOPK)[None, :, None] > jnp.arange(TOPK)[None, None, :]
    )
    rank = rank + jnp.sum(twin.astype(f32), axis=2)
    return ids.astype(f32), rank


def spread(slots, values, sent):
    row_ids = jnp.arange(sent, dtype=f32)[:, None]
    total = jnp.zeros((sent, slots.shape[1]), f32)
    for k in range(TOPK):
        total = total + jnp.where(slots[k][None, :] == row_ids, values[k][None, :], 0.0)
    return total.astype(bf16)


def packing(used, group):
    place = np.arange(PEERS * used)
    return (place // used * group + place % used)[:, None] == np.arange(PEERS * group)[None, :]


def products_kernel(
    used, group, own_ref, other_ref, w_own_ref, w_other_ref, inv_own_ref, inv_other_ref, pick_ref, part_ref
):
    share, pack = 2 * PEERS * used, PEERS * group
    lanes = -(-share // 128) * 128
    ones = jnp.ones((8, SLICE), bf16)
    row = lax.broadcasted_iota(jnp.int32, (EXTRA, FF), 0)

    def packed(ref, h):
        if used == group:
            return ref[h * share : (h + 1) * share].astype(f32)
        pick = pick_ref[...]
        halves = [
            jnp.dot(
                pick,
                ref[(2 * h + i) * pack : (2 * h + i + 1) * pack],
                preferred_element_type=f32,
            )
            for i in range(2)
        ]
        return jnp.concatenate(halves, axis=0)

    def squares(rows, inverse_ref):
        weighted = (rows * rows * inverse_ref[...]).astype(bf16)
        if lanes > share:
            weighted = jnp.concatenate(
                [weighted, jnp.zeros((lanes - share, SLICE), bf16)], axis=0
            )
        return lax.dot_general(
            ones, weighted, (((1,), (1,)), ((), ())), preferred_element_type=f32
        )

    for h in range(NH):
        own, other = packed(own_ref, h), packed(other_ref, h)
        part = jnp.dot(own.astype(bf16), w_own_ref[...], preferred_element_type=f32) + jnp.dot(
            other.astype(bf16), w_other_ref[...], preferred_element_type=f32
        )
        total = squares(own, inv_own_ref) + squares(other, inv_other_ref)
        total = jnp.concatenate([total, jnp.zeros((8, FF - lanes), f32)], axis=1)
        high = total.astype(bf16).astype(f32)
        tail = jnp.where(row == 0, high, jnp.where(row == 1, total - high, 0.0))
        part_ref[h] = jnp.concatenate([part, tail], axis=0).astype(bf16)


def products(used, group, own, other, w_own, w_other, inv_own, inv_other):
    return pl.pallas_call(
        functools.partial(products_kernel, used, group),
        out_shape=jax.ShapeDtypeStruct((NH, 2 * PEERS * used + EXTRA, FF), bf16),
        compiler_params=pltpu.CompilerParams(vmem_limit_bytes=48 * 1024 * 1024),
        cost_estimate=pl.CostEstimate(flops=100_000_000, bytes_accessed=500_000, transcendentals=0),
    )(own, other, w_own, w_other, inv_own, inv_other, jnp.asarray(packing(used, group), bf16))


def results_kernel(used, group, own_ref, other_ref, down_own_ref, down_other_ref, place_ref, out_ref):
    share, pack = 2 * PEERS * used, PEERS * group
    for h in range(NH):
        rows = slice(h * share, (h + 1) * share)
        part = jnp.dot(own_ref[rows], down_own_ref[...], preferred_element_type=f32) + jnp.dot(
            other_ref[rows], down_other_ref[...], preferred_element_type=f32
        )
        if used == group:
            out_ref[rows] = part.astype(bf16)
            continue
        for i in range(2):
            rows = part[i * PEERS * used : (i + 1) * PEERS * used].astype(bf16)
            start = (2 * h + i) * pack
            out_ref[start : start + pack] = jnp.dot(
                place_ref[...], rows, preferred_element_type=f32
            ).astype(bf16)


def expert_results(used, group, own, other, down_own, down_other):
    return pl.pallas_call(
        functools.partial(results_kernel, used, group),
        out_shape=jax.ShapeDtypeStruct((N_CTX * group, SLICE), bf16),
        compiler_params=pltpu.CompilerParams(vmem_limit_bytes=48 * 1024 * 1024),
        cost_estimate=pl.CostEstimate(flops=100_000_000, bytes_accessed=500_000, transcendentals=0),
    )(own, other, down_own, down_other, jnp.asarray(packing(used, group).T, bf16))


def body(
    queries,
    key_rows,
    value_rows,
    out_weight,
    residual,
    norm_gain,
    w_gate,
    w_up,
    w_down,
    pred_ids,
    route_gates,
    fix_pair,
    fix_expert,
    fix_count,
):
    core, side = lax.axis_index("c"), lax.axis_index("l")
    tokens = queries.shape[0]
    half = FF // 2

    other_strip = swap(out_weight, "l")
    strips = jnp.where(
        side == 0,
        jnp.concatenate([out_weight, other_strip], axis=0),
        jnp.concatenate([other_strip, out_weight], axis=0),
    )
    strips, queries = lax.optimization_barrier((strips, queries))
    quarter = lax.all_gather(strips, "y", axis=0, tiled=True)

    attended = attention(queries, key_rows, value_rows)
    heads = exchange(jnp.broadcast_to(attended[None], (NH, *attended.shape)), "h")
    heads = exchange(heads, "x").reshape(NX * tokens, SLICE)
    other_heads = swap(heads, "c")
    partial = jnp.dot(
        heads,
        lax.dynamic_slice_in_dim(quarter, core * SLICE, SLICE, 0),
        preferred_element_type=f32,
    ) + jnp.dot(
        other_heads,
        lax.dynamic_slice_in_dim(quarter, (1 - core) * SLICE, SLICE, 0),
        preferred_element_type=f32,
    )
    partial, pred_ids, fix_pair, fix_count, w_gate, w_up, norm_gain = lax.optimization_barrier(
        (partial.astype(bf16), pred_ids, fix_pair, fix_count, w_gate, w_up, norm_gain)
    )

    ids, rank = slots_of(pred_ids, fix_pair, fix_expert, fix_count)
    ids, rank, gates = ids.T, rank.T, route_gates.astype(f32).T
    lists = [
        jnp.where((rank >= first) & (rank < first + used), ids * group + rank - first, -1.0)
        for first, used, group in PARTS
    ]
    picks = [
        spread(slots, jnp.ones_like(slots), N_CTX * part[2]) for slots, part in zip(lists, PARTS)
    ]

    def columns(which):
        return jnp.concatenate(
            [
                lax.dynamic_slice_in_dim(w_gate[0], which * half, half, 1),
                lax.dynamic_slice_in_dim(w_up[0], which * half, half, 1),
            ],
            axis=1,
        )

    gate_up, other_gate_up = columns(core), swap(columns(1 - core), "c")
    down = lax.dynamic_slice_in_dim(w_down[0], core * half, half, 0)
    other_down = lax.dynamic_slice_in_dim(w_down[0], (1 - core) * half, half, 0)
    gain = norm_gain[None, :]
    inverse = 1.0 / (gain * gain)
    other_inverse = swap(inverse, "c")

    terms = exchange(partial.reshape(NX, tokens, SLICE), "x")
    terms, pick = lax.optimization_barrier((terms, picks[0]))
    stream = residual.astype(f32) + jnp.sum(terms.astype(f32), axis=0)

    scaled = (stream * gain).astype(bf16)

    def through(part, rows):
        group = PARTS[part][2]
        return exchange(rows.reshape(N_CTX, group, SLICE), CTX).reshape(N_CTX * group, SLICE)

    def sent(part, pick):
        return through(part, jnp.dot(pick, scaled, preferred_element_type=f32).astype(bf16))

    def reduced(part, rows):
        sums = products(
            *PARTS[part][1:], rows, swap(rows, "c"), gate_up, other_gate_up, inverse, other_inverse
        )
        return lax.psum_scatter(
            sums.reshape(-1, FF), "h", scatter_dimension=0, tiled=True
        )

    def gathered(part, sums):
        share = 2 * PEERS * PARTS[part][1]
        sums = sums.astype(f32)
        total = (sums[share] + sums[share + 1])[:share]
        sums = sums[:share] * lax.rsqrt(total / D + epsilon)[:, None]
        hidden = (jax.nn.silu(sums[:, :half]) * sums[:, half:]).astype(bf16)
        return lax.all_gather(hidden, "h", axis=0, tiled=True)

    def finished(part, hidden):
        rows = expert_results(*PARTS[part][1:], hidden, swap(hidden, "c"), down, other_down)
        return through(part, rows)

    def combined(combine, rows):
        return jnp.einsum("rt,rd->td", combine, rows, preferred_element_type=f32)

    first = sent(0, pick)
    first, other_pick, gate_up, other_gate_up, inverse, other_inverse = lax.optimization_barrier(
        (first, picks[1], gate_up, other_gate_up, inverse, other_inverse)
    )
    first = reduced(0, first)
    second = sent(1, other_pick)
    first, second = lax.optimization_barrier((first, second))
    second = reduced(1, second)
    first = finished(0, gathered(0, first))
    hidden = gathered(1, second)
    combine = spread(lists[1], gates, N_CTX * PARTS[1][2])
    first, hidden, combine = lax.optimization_barrier((first, hidden, combine))
    second = finished(1, hidden)
    expert_out = combined(spread(lists[0], gates, N_CTX * PARTS[0][2]), first)
    expert_out = expert_out + combined(combine, second)
    return stream.astype(bf16), expert_out.astype(bf16)


def solution(mesh):
    split = Mesh(np.asarray(mesh.devices).reshape(NX, NY, NL, NH, NC), ("x", "y", "l", "h", "c"))
    ctx, exp = CTX, ("h", "c")
    placed = (
        P(ctx, exp),
        P(ctx, None),
        P(ctx, None),
        P(ctx, exp),
        P(ctx, exp),
        P(exp),
        P(ctx, exp, None),
        P(ctx, exp, None),
        P(ctx, None, exp),
        P(ctx, None),
        P(ctx, None),
        P(ctx, None),
        P(ctx, None),
        P(ctx),
    )
    return jax.shard_map(
        body,
        mesh=split,
        in_specs=placed,
        out_specs=(P(ctx, exp), P(ctx, exp)),
        check_vma=False,
    )
```

```python
import jax
import jax.numpy as jnp
import numpy as np
from jax import lax
from jax.experimental import pallas as pl
from jax.experimental.pallas import tpu as pltpu
from jax.sharding import Mesh, PartitionSpec as P

D = 4096
HD = 128
TOPK = 8
QH = 32
KVH = 2
FF = 768
FIX = 32
TOK = 128
SLOTS = 21
GROUP = 24
NX, NY, NL, NH, NC = 4, 8, 2, 4, 2
N_CTX = NX * NY * NL
GRID = NX * NY
SENT = GRID * GROUP
ROWS = GRID * SLOTS
SHARE = ROWS // NH
LANES = 256
EXTRA = 8
PACK = 8 * SLOTS
PACK_SENT = 8 * GROUP
SLICE = D // (NH * NC)
CTX = ("x", "y", "l")
f32, bf16 = jnp.float32, jnp.bfloat16

epsilon = 1e-06


def swap(block, axis):
    return lax.ppermute(block, axis, [(0, 1), (1, 0)])


def exchange(blocks, axes):
    return lax.all_to_all(blocks, axes, split_axis=0, concat_axis=0, tiled=True)


def from_behind(block, distance):
    route = [(i, i + distance) for i in range(N_CTX - distance)]
    return lax.ppermute(block, CTX, route)


def attention(queries, key_rows, value_rows):
    tokens = queries.shape[0]
    block = lax.axis_index(CTX)
    kv_first = lax.axis_index("h") // 2 * HD
    own = jnp.concatenate(
        [
            lax.dynamic_slice_in_dim(key_rows, kv_first, HD, 1),
            lax.dynamic_slice_in_dim(value_rows, kv_first, HD, 1),
        ],
        axis=1,
    )
    pairs = [from_behind(own, 3), from_behind(own, 2), from_behind(own, 1), own]
    keys = jnp.concatenate([pair[:, :HD] for pair in pairs], axis=0)
    values = jnp.concatenate([pair[:, HD:] for pair in pairs], axis=0)
    q_view = queries.reshape(tokens, -1, HD)
    scores = jnp.einsum("tgd,sd->gts", q_view, keys, preferred_element_type=f32) / HD**0.5
    q_pos = block * tokens + jnp.arange(tokens)
    k_pos = (block - 3) * tokens + jnp.arange(4 * tokens)
    allowed = (k_pos[None, :] >= 0) & (k_pos[None, :] <= q_pos[:, None])
    scores = jnp.where(allowed, scores, -1e30)
    highest = jnp.max(scores, axis=2, keepdims=True)
    weights = jnp.where(allowed, jnp.exp(scores - highest), 0.0)
    denominators = jnp.sum(weights, axis=2, keepdims=True)
    mixed = (
        jnp.einsum("gts,sd->gtd", weights.astype(bf16), values, preferred_element_type=f32)
        / denominators
    )
    return jnp.transpose(mixed, (1, 0, 2)).reshape(tokens, -1).astype(bf16)


def slots_of(pred_ids, fix_pair, fix_expert, fix_count):
    tokens = pred_ids.shape[0]
    places = jnp.arange(tokens * TOPK, dtype=jnp.int32).reshape(tokens, TOPK)
    live = jnp.arange(FIX) < fix_count[0]
    hit = (places[:, :, None] == fix_pair[0][None, None, :]) & live[None, None, :]
    fixed = jnp.sum(jnp.where(hit, fix_expert[0][None, None, :], 0), axis=2)
    ids = jnp.where(jnp.any(hit, axis=2), fixed, pred_ids)
    named = ids[:, :, None] == jnp.arange(N_CTX)[None, None, :]
    counts = jnp.sum(named.astype(f32), axis=1)
    earlier = (
        jnp.arange(tokens)[:, None] > jnp.arange(tokens)[None, :]
    ).astype(bf16)
    before = jnp.dot(earlier, counts.astype(bf16), preferred_element_type=f32)
    rank = jnp.sum(jnp.where(named, before[:, None, :], 0.0), axis=2)
    twin = (ids[:, :, None] == ids[:, None, :]) & (
        jnp.arange(TOPK)[None, :, None] > jnp.arange(TOPK)[None, None, :]
    )
    rank = rank + jnp.sum(twin.astype(f32), axis=2)
    return ids.astype(f32), rank


def row_slots(table, side):
    ids, rank, gates = table[:TOPK], table[TOPK : 2 * TOPK], table[2 * TOPK :]
    column = jnp.floor(ids * 0.5)
    return jnp.where(ids - 2.0 * column == side, column * GROUP + rank, -1.0), gates


def spread(slots, values):
    row_ids = jnp.arange(SENT, dtype=f32)[:, None]
    total = jnp.zeros((SENT, slots.shape[1]), f32)
    for k in range(TOPK):
        total = total + jnp.where(slots[k][None, :] == row_ids, values[k][None, :], 0.0)
    return total.astype(bf16)


def packing():
    place = np.arange(PACK)
    return (place // SLOTS * GROUP + place % SLOTS)[:, None] == np.arange(PACK_SENT)[None, :]


def products_kernel(
    own_ref, other_ref, w_own_ref, w_other_ref, inv_own_ref, inv_other_ref, pick_ref, part_ref
):
    pick = pick_ref[...]
    ones = jnp.ones((8, SLICE), bf16)
    blank = jnp.zeros((LANES - SHARE, SLICE), bf16)
    row = lax.broadcasted_iota(jnp.int32, (EXTRA, FF), 0)

    def squares(rows, inverse_ref):
        weighted = (rows * rows * inverse_ref[...]).astype(bf16)
        return lax.dot_general(
            ones,
            jnp.concatenate([weighted, blank], axis=0),
            (((1,), (1,)), ((), ())),
            preferred_element_type=f32,
        )

    for h in range(NH):
        taken = slice(h * PACK_SENT, (h + 1) * PACK_SENT)
        own = jnp.dot(pick, own_ref[taken], preferred_element_type=f32)
        other = jnp.dot(pick, other_ref[taken], preferred_element_type=f32)
        part = jnp.dot(own.astype(bf16), w_own_ref[...], preferred_element_type=f32) + jnp.dot(
            other.astype(bf16), w_other_ref[...], preferred_element_type=f32
        )
        total = squares(own, inv_own_ref) + squares(other, inv_other_ref)
        total = jnp.concatenate([total, jnp.zeros((8, FF - LANES), f32)], axis=1)
        high = total.astype(bf16).astype(f32)
        tail = jnp.where(row == 0, high, jnp.where(row == 1, total - high, 0.0))
        part_ref[h] = jnp.concatenate([part, tail], axis=0).astype(bf16)


def products(own, other, w_own, w_other, inv_own, inv_other):
    return pl.pallas_call(
        products_kernel,
        out_shape=jax.ShapeDtypeStruct((NH, SHARE + EXTRA, FF), bf16),
        compiler_params=pltpu.CompilerParams(vmem_limit_bytes=48 * 1024 * 1024),
        cost_estimate=pl.CostEstimate(flops=100_000_000, bytes_accessed=500_000, transcendentals=0),
    )(own, other, w_own, w_other, inv_own, inv_other, jnp.asarray(packing(), bf16))


def results_kernel(own_ref, other_ref, down_own_ref, down_other_ref, place_ref, out_ref):
    place = place_ref[...]
    for i in range(NH // 2):
        rows = slice(2 * i * SHARE, 2 * (i + 1) * SHARE)
        part = jnp.dot(own_ref[rows], down_own_ref[...], preferred_element_type=f32) + jnp.dot(
            other_ref[rows], down_other_ref[...], preferred_element_type=f32
        )
        for j in range(2):
            rows = part[j * PACK : (j + 1) * PACK].astype(bf16)
            start = (2 * i + j) * PACK_SENT
            out_ref[start : start + PACK_SENT] = jnp.dot(
                place, rows, preferred_element_type=f32
            ).astype(bf16)


def expert_results(own, other, down_own, down_other):
    return pl.pallas_call(
        results_kernel,
        out_shape=jax.ShapeDtypeStruct((SENT, SLICE), bf16),
        compiler_params=pltpu.CompilerParams(vmem_limit_bytes=48 * 1024 * 1024),
        cost_estimate=pl.CostEstimate(flops=100_000_000, bytes_accessed=500_000, transcendentals=0),
    )(own, other, down_own, down_other, jnp.asarray(packing().T, bf16))


def body(
    queries,
    key_rows,
    value_rows,
    out_weight,
    residual,
    norm_gain,
    w_gate,
    w_up,
    w_down,
    pred_ids,
    route_gates,
    fix_pair,
    fix_expert,
    fix_count,
):
    core, side = lax.axis_index("c"), lax.axis_index("l")
    tokens = queries.shape[0]
    half = FF // 2

    attended = attention(queries, key_rows, value_rows)

    other_strip = swap(out_weight, "l")
    attended, other_strip = lax.optimization_barrier((attended, other_strip))
    strips = jnp.where(
        side == 0,
        jnp.concatenate([out_weight, other_strip], axis=0),
        jnp.concatenate([other_strip, out_weight], axis=0),
    )
    strips, attended = lax.optimization_barrier((strips, attended))
    quarter = lax.all_gather(strips, "y", axis=0, tiled=True)

    attended, pred_ids, fix_pair = lax.optimization_barrier((attended, pred_ids, fix_pair))
    ids, rank = slots_of(pred_ids, fix_pair, fix_expert, fix_count)
    table = jnp.concatenate([ids, rank, route_gates.astype(f32)], axis=1)
    slots, gates = row_slots(table.T, side.astype(f32))
    pick = spread(slots, jnp.ones_like(slots))

    heads = exchange(jnp.broadcast_to(attended[None], (NH, *attended.shape)), "h")
    other_slots, other_gates = row_slots(swap(table, "l").T, side.astype(f32))
    heads = exchange(heads, "x").reshape(NX * tokens, SLICE)
    heads, other_slots = lax.optimization_barrier((heads, other_slots))
    other_heads = swap(heads, "c")
    partial = jnp.dot(
        heads,
        lax.dynamic_slice_in_dim(quarter, core * SLICE, SLICE, 0),
        preferred_element_type=f32,
    ) + jnp.dot(
        other_heads,
        lax.dynamic_slice_in_dim(quarter, (1 - core) * SLICE, SLICE, 0),
        preferred_element_type=f32,
    )
    partial, w_gate, w_up, norm_gain = lax.optimization_barrier(
        (partial.astype(bf16), w_gate, w_up, norm_gain)
    )

    def columns(which):
        return jnp.concatenate(
            [
                lax.dynamic_slice_in_dim(w_gate[0], which * half, half, 1),
                lax.dynamic_slice_in_dim(w_up[0], which * half, half, 1),
            ],
            axis=1,
        )

    gate_up, other_gate_up = columns(core), swap(columns(1 - core), "c")
    down = lax.dynamic_slice_in_dim(w_down[0], core * half, half, 0)
    other_down = lax.dynamic_slice_in_dim(w_down[0], (1 - core) * half, half, 0)
    gain = norm_gain[None, :]
    inverse = 1.0 / (gain * gain)
    other_inverse = swap(inverse, "c")

    terms = exchange(partial.reshape(NX, tokens, SLICE), "x")
    other_pick = spread(other_slots, jnp.ones_like(other_slots))
    terms, other_pick = lax.optimization_barrier((terms, other_pick))
    stream = residual.astype(f32) + jnp.sum(terms.astype(f32), axis=0)

    scaled = (stream * gain).astype(bf16)
    beside = swap(scaled, "l")

    def through(rows):
        return exchange(rows.reshape(GRID, GROUP, SLICE), ("x", "y")).reshape(SENT, SLICE)

    def sent(pick, rows):
        return through(jnp.dot(pick, rows, preferred_element_type=f32).astype(bf16))

    def share_products(rows):
        return products(rows, swap(rows, "c"), gate_up, other_gate_up, inverse, other_inverse)

    def reduced(part):
        flat = part.reshape(NH * (SHARE + EXTRA), FF)
        return lax.psum_scatter(flat, "h", scatter_dimension=0, tiled=True)

    def gathered(sums):
        sums = sums.astype(f32)
        total = (sums[SHARE] + sums[SHARE + 1])[:SHARE]
        sums = sums[:SHARE] * lax.rsqrt(total / D + epsilon)[:, None]
        hidden = (jax.nn.silu(sums[:, :half]) * sums[:, half:]).astype(bf16)
        return lax.all_gather(hidden, "h", axis=0, tiled=True)

    def finished(hidden):
        return expert_results(hidden, swap(hidden, "c"), down, other_down)

    first = sent(other_pick, beside)
    first, pick, gate_up, other_gate_up, inverse, other_inverse = lax.optimization_barrier(
        (first, pick, gate_up, other_gate_up, inverse, other_inverse)
    )
    first = reduced(share_products(first))
    second = sent(pick, scaled)
    first, second = lax.optimization_barrier((first, second))
    second = reduced(share_products(second))
    first = through(finished(gathered(first)))
    hidden = gathered(second)
    combine = spread(slots, gates)
    first, hidden, combine = lax.optimization_barrier((first, hidden, combine))
    second = through(finished(hidden))
    other_mixed = jnp.einsum(
        "rt,rd->td", spread(other_slots, other_gates), first, preferred_element_type=f32
    )
    mixed = jnp.einsum("rt,rd->td", combine, second, preferred_element_type=f32)
    expert_out = mixed + swap(other_mixed.astype(bf16), "l").astype(f32)
    return stream.astype(bf16), expert_out.astype(bf16)


def solution(mesh):
    split = Mesh(np.asarray(mesh.devices).reshape(NX, NY, NL, NH, NC), ("x", "y", "l", "h", "c"))
    ctx, exp = CTX, ("h", "c")
    placed = (
        P(ctx, exp),
        P(ctx, None),
        P(ctx, None),
        P(ctx, exp),
        P(ctx, exp),
        P(exp),
        P(ctx, exp, None),
        P(ctx, exp, None),
        P(ctx, None, exp),
        P(ctx, None),
        P(ctx, None),
        P(ctx, None),
        P(ctx, None),
        P(ctx),
    )
    return jax.shard_map(
        body,
        mesh=split,
        in_specs=placed,
        out_specs=(P(ctx, exp), P(ctx, exp)),
        check_vma=False,
    )
```

```python
import jax
import jax.numpy as jnp
import numpy as np
from jax import lax
from jax.experimental import pallas as pl
from jax.experimental.pallas import tpu as pltpu
from jax.sharding import Mesh, PartitionSpec as P

D = 4096
HD = 128
TOPK = 8
QH = 32
KVH = 2
FF = 768
FIX = 32
TOK = 128
SLOTS = 21
GROUP = 24
NX, NY, NL, NH, NC = 4, 8, 2, 4, 2
N_CTX = NX * NY * NL
GRID = NX * NY
SENT = GRID * GROUP
ROWS = GRID * SLOTS
SHARE = ROWS // NH
LANES = 256
EXTRA = 8
PACK = 8 * SLOTS
PACK_SENT = 8 * GROUP
SLICE = D // (NH * NC)
CTX = ("x", "y", "l")
f32, bf16 = jnp.float32, jnp.bfloat16

epsilon = 1e-06


def swap(block, axis):
    return lax.ppermute(block, axis, [(0, 1), (1, 0)])


def exchange(blocks, axes):
    return lax.all_to_all(blocks, axes, split_axis=0, concat_axis=0, tiled=True)


def from_behind(block, distance):
    route = [(i, i + distance) for i in range(N_CTX - distance)]
    return lax.ppermute(block, CTX, route)


def attention(queries, key_rows, value_rows):
    tokens = queries.shape[0]
    block = lax.axis_index(CTX)
    kv_first = lax.axis_index("h") // 2 * HD
    own = jnp.concatenate(
        [
            lax.dynamic_slice_in_dim(key_rows, kv_first, HD, 1),
            lax.dynamic_slice_in_dim(value_rows, kv_first, HD, 1),
        ],
        axis=1,
    )
    pairs = [from_behind(own, 3), from_behind(own, 2), from_behind(own, 1), own]
    keys = jnp.concatenate([pair[:, :HD] for pair in pairs], axis=0)
    values = jnp.concatenate([pair[:, HD:] for pair in pairs], axis=0)
    q_view = queries.reshape(tokens, -1, HD)
    scores = jnp.einsum("tgd,sd->gts", q_view, keys, preferred_element_type=f32) / HD**0.5
    q_pos = block * tokens + jnp.arange(tokens)
    k_pos = (block - 3) * tokens + jnp.arange(4 * tokens)
    allowed = (k_pos[None, :] >= 0) & (k_pos[None, :] <= q_pos[:, None])
    scores = jnp.where(allowed, scores, -1e30)
    highest = jnp.max(scores, axis=2, keepdims=True)
    weights = jnp.where(allowed, jnp.exp(scores - highest), 0.0)
    denominators = jnp.sum(weights, axis=2, keepdims=True)
    mixed = (
        jnp.einsum("gts,sd->gtd", weights.astype(bf16), values, preferred_element_type=f32)
        / denominators
    )
    return jnp.transpose(mixed, (1, 0, 2)).reshape(tokens, -1).astype(bf16)


def slots_of(pred_ids, fix_pair, fix_expert, fix_count):
    tokens = pred_ids.shape[0]
    places = jnp.arange(tokens * TOPK, dtype=jnp.int32).reshape(tokens, TOPK)
    live = jnp.arange(FIX) < fix_count[0]
    hit = (places[:, :, None] == fix_pair[0][None, None, :]) & live[None, None, :]
    fixed = jnp.sum(jnp.where(hit, fix_expert[0][None, None, :], 0), axis=2)
    ids = jnp.where(jnp.any(hit, axis=2), fixed, pred_ids)
    named = ids[:, :, None] == jnp.arange(N_CTX)[None, None, :]
    counts = jnp.sum(named.astype(f32), axis=1)
    earlier = (
        jnp.arange(tokens)[:, None] > jnp.arange(tokens)[None, :]
    ).astype(bf16)
    before = jnp.dot(earlier, counts.astype(bf16), preferred_element_type=f32)
    rank = jnp.sum(jnp.where(named, before[:, None, :], 0.0), axis=2)
    twin = (ids[:, :, None] == ids[:, None, :]) & (
        jnp.arange(TOPK)[None, :, None] > jnp.arange(TOPK)[None, None, :]
    )
    rank = rank + jnp.sum(twin.astype(f32), axis=2)
    return ids.astype(f32), rank


def row_slots(table, side):
    ids, rank, gates = table[:TOPK], table[TOPK : 2 * TOPK], table[2 * TOPK :]
    column = jnp.floor(ids * 0.5)
    return jnp.where(ids - 2.0 * column == side, column * GROUP + rank, -1.0), gates


def spread(slots, values):
    row_ids = jnp.arange(SENT, dtype=f32)[:, None]
    total = jnp.zeros((SENT, slots.shape[1]), f32)
    for k in range(TOPK):
        total = total + jnp.where(slots[k][None, :] == row_ids, values[k][None, :], 0.0)
    return total.astype(bf16)


def packing():
    place = np.arange(PACK)
    return (place // SLOTS * GROUP + place % SLOTS)[:, None] == np.arange(PACK_SENT)[None, :]


def products_kernel(
    own_ref, other_ref, w_own_ref, w_other_ref, inv_own_ref, inv_other_ref, pick_ref, part_ref
):
    pick = pick_ref[...]
    ones = jnp.ones((8, SLICE), bf16)
    blank = jnp.zeros((LANES - SHARE, SLICE), bf16)
    row = lax.broadcasted_iota(jnp.int32, (EXTRA, FF), 0)

    def squares(rows, inverse_ref):
        weighted = (rows * rows * inverse_ref[...]).astype(bf16)
        return lax.dot_general(
            ones,
            jnp.concatenate([weighted, blank], axis=0),
            (((1,), (1,)), ((), ())),
            preferred_element_type=f32,
        )

    for h in range(NH):
        taken = slice(h * PACK_SENT, (h + 1) * PACK_SENT)
        own = jnp.dot(pick, own_ref[taken], preferred_element_type=f32)
        other = jnp.dot(pick, other_ref[taken], preferred_element_type=f32)
        part = jnp.dot(own.astype(bf16), w_own_ref[...], preferred_element_type=f32) + jnp.dot(
            other.astype(bf16), w_other_ref[...], preferred_element_type=f32
        )
        total = squares(own, inv_own_ref) + squares(other, inv_other_ref)
        total = jnp.concatenate([total, jnp.zeros((8, FF - LANES), f32)], axis=1)
        high = total.astype(bf16).astype(f32)
        tail = jnp.where(row == 0, high, jnp.where(row == 1, total - high, 0.0))
        part_ref[h] = jnp.concatenate([part, tail], axis=0).astype(bf16)


def products(own, other, w_own, w_other, inv_own, inv_other):
    return pl.pallas_call(
        products_kernel,
        out_shape=jax.ShapeDtypeStruct((NH, SHARE + EXTRA, FF), bf16),
        compiler_params=pltpu.CompilerParams(vmem_limit_bytes=48 * 1024 * 1024),
        cost_estimate=pl.CostEstimate(flops=100_000_000, bytes_accessed=500_000, transcendentals=0),
    )(own, other, w_own, w_other, inv_own, inv_other, jnp.asarray(packing(), bf16))


def results_kernel(own_ref, other_ref, down_own_ref, down_other_ref, place_ref, out_ref):
    place = place_ref[...]
    for i in range(NH // 2):
        rows = slice(2 * i * SHARE, 2 * (i + 1) * SHARE)
        part = jnp.dot(own_ref[rows], down_own_ref[...], preferred_element_type=f32) + jnp.dot(
            other_ref[rows], down_other_ref[...], preferred_element_type=f32
        )
        for j in range(2):
            rows = part[j * PACK : (j + 1) * PACK].astype(bf16)
            start = (2 * i + j) * PACK_SENT
            out_ref[start : start + PACK_SENT] = jnp.dot(
                place, rows, preferred_element_type=f32
            ).astype(bf16)


def expert_results(own, other, down_own, down_other):
    return pl.pallas_call(
        results_kernel,
        out_shape=jax.ShapeDtypeStruct((SENT, SLICE), bf16),
        compiler_params=pltpu.CompilerParams(vmem_limit_bytes=48 * 1024 * 1024),
        cost_estimate=pl.CostEstimate(flops=100_000_000, bytes_accessed=500_000, transcendentals=0),
    )(own, other, down_own, down_other, jnp.asarray(packing().T, bf16))


def activation_kernel(sums_ref, hidden_ref):
    sums = sums_ref[...].astype(f32)
    total = sums[SHARE : SHARE + 1, :LANES] + sums[SHARE + 1 : SHARE + 2, :LANES]
    scale = lax.rsqrt(total / D + epsilon)
    at = lax.broadcasted_iota(jnp.int32, (SHARE, LANES), 0)
    lane = lax.broadcasted_iota(jnp.int32, (SHARE, LANES), 1)
    scale = jnp.sum(jnp.where(at == lane, scale, 0.0), axis=1, keepdims=True)
    gate, up = sums[:SHARE, : FF // 2] * scale, sums[:SHARE, FF // 2 :] * scale
    hidden_ref[...] = (gate / (1.0 + jnp.exp(-gate)) * up).astype(bf16)


def activated(sums):
    return pl.pallas_call(
        activation_kernel,
        out_shape=jax.ShapeDtypeStruct((SHARE, FF // 2), bf16),
        compiler_params=pltpu.CompilerParams(vmem_limit_bytes=32 * 1024 * 1024),
        cost_estimate=pl.CostEstimate(flops=1_000_000, bytes_accessed=100_000, transcendentals=0),
    )(sums)


def body(
    queries,
    key_rows,
    value_rows,
    out_weight,
    residual,
    norm_gain,
    w_gate,
    w_up,
    w_down,
    pred_ids,
    route_gates,
    fix_pair,
    fix_expert,
    fix_count,
):
    core, side = lax.axis_index("c"), lax.axis_index("l")
    tokens = queries.shape[0]
    half = FF // 2

    attended = attention(queries, key_rows, value_rows)

    other_strip = swap(out_weight, "l")
    attended, other_strip = lax.optimization_barrier((attended, other_strip))
    strips = jnp.where(
        side == 0,
        jnp.concatenate([out_weight, other_strip], axis=0),
        jnp.concatenate([other_strip, out_weight], axis=0),
    )
    strips, attended = lax.optimization_barrier((strips, attended))
    quarter = lax.all_gather(strips, "y", axis=0, tiled=True)

    attended, pred_ids, fix_pair = lax.optimization_barrier((attended, pred_ids, fix_pair))
    ids, rank = slots_of(pred_ids, fix_pair, fix_expert, fix_count)
    table = jnp.concatenate([ids, rank, route_gates.astype(f32)], axis=1)
    slots, gates = row_slots(table.T, side.astype(f32))
    pick = spread(slots, jnp.ones_like(slots))

    heads = lax.all_gather(attended, "h", axis=0, tiled=True).reshape(NH, tokens, SLICE)
    other_slots, other_gates = row_slots(swap(table, "l").T, side.astype(f32))
    heads = exchange(heads, "x").reshape(NX * tokens, SLICE)
    heads, other_slots = lax.optimization_barrier((heads, other_slots))
    other_heads = swap(heads, "c")
    partial = jnp.dot(
        heads,
        lax.dynamic_slice_in_dim(quarter, core * SLICE, SLICE, 0),
        preferred_element_type=f32,
    ) + jnp.dot(
        other_heads,
        lax.dynamic_slice_in_dim(quarter, (1 - core) * SLICE, SLICE, 0),
        preferred_element_type=f32,
    )
    partial, w_gate, w_up, norm_gain = lax.optimization_barrier(
        (partial.astype(bf16), w_gate, w_up, norm_gain)
    )

    def columns(which):
        return jnp.concatenate(
            [
                lax.dynamic_slice_in_dim(w_gate[0], which * half, half, 1),
                lax.dynamic_slice_in_dim(w_up[0], which * half, half, 1),
            ],
            axis=1,
        )

    gate_up, other_gate_up = columns(core), swap(columns(1 - core), "c")
    down = lax.dynamic_slice_in_dim(w_down[0], core * half, half, 0)
    other_down = lax.dynamic_slice_in_dim(w_down[0], (1 - core) * half, half, 0)
    gain = norm_gain[None, :]
    inverse = 1.0 / (gain * gain)
    other_inverse = swap(inverse, "c")

    terms = exchange(partial.reshape(NX, tokens, SLICE), "x")
    other_pick = spread(other_slots, jnp.ones_like(other_slots))
    terms, other_pick = lax.optimization_barrier((terms, other_pick))
    stream = residual.astype(f32) + jnp.sum(terms.astype(f32), axis=0)

    scaled = (stream * gain).astype(bf16)
    beside = swap(scaled, "l")

    def through(rows):
        return exchange(rows.reshape(GRID, GROUP, SLICE), ("x", "y")).reshape(SENT, SLICE)

    def sent(pick, rows):
        return through(jnp.dot(pick, rows, preferred_element_type=f32).astype(bf16))

    def share_products(rows):
        return products(rows, swap(rows, "c"), gate_up, other_gate_up, inverse, other_inverse)

    def reduced(part):
        flat = part.reshape(NH * (SHARE + EXTRA), FF)
        return lax.psum_scatter(flat, "h", scatter_dimension=0, tiled=True)

    def gathered(sums):
        return lax.all_gather(activated(sums), "h", axis=0, tiled=True)

    def finished(hidden):
        return expert_results(hidden, swap(hidden, "c"), down, other_down)

    first = sent(other_pick, beside)
    first, pick, gate_up, other_gate_up, inverse, other_inverse = lax.optimization_barrier(
        (first, pick, gate_up, other_gate_up, inverse, other_inverse)
    )
    first = reduced(share_products(first))
    second = sent(pick, scaled)
    first, second = lax.optimization_barrier((first, second))
    second = reduced(share_products(second))
    first = through(finished(gathered(first)))
    hidden = gathered(second)
    combine = spread(slots, gates)
    first, hidden, combine = lax.optimization_barrier((first, hidden, combine))
    second = through(finished(hidden))
    other_mixed = jnp.einsum(
        "rt,rd->td", spread(other_slots, other_gates), first, preferred_element_type=f32
    )
    mixed = jnp.einsum("rt,rd->td", combine, second, preferred_element_type=f32)
    expert_out = mixed + swap(other_mixed.astype(bf16), "l").astype(f32)
    return stream.astype(bf16), expert_out.astype(bf16)


def solution(mesh):
    split = Mesh(np.asarray(mesh.devices).reshape(NX, NY, NL, NH, NC), ("x", "y", "l", "h", "c"))
    ctx, exp = CTX, ("h", "c")
    placed = (
        P(ctx, exp),
        P(ctx, None),
        P(ctx, None),
        P(ctx, exp),
        P(ctx, exp),
        P(exp),
        P(ctx, exp, None),
        P(ctx, exp, None),
        P(ctx, None, exp),
        P(ctx, None),
        P(ctx, None),
        P(ctx, None),
        P(ctx, None),
        P(ctx),
    )
    return jax.shard_map(
        body,
        mesh=split,
        in_specs=placed,
        out_specs=(P(ctx, exp), P(ctx, exp)),
        check_vma=False,
    )
```

```python
import jax
import jax.numpy as jnp
import numpy as np
from jax import lax
from jax.experimental import pallas as pl
from jax.experimental.pallas import tpu as pltpu
from jax.sharding import Mesh, PartitionSpec as P

D = 4096
HD = 128
TOPK = 8
QH = 32
KVH = 2
FF = 768
FIX = 32
TOK = 128
SLOTS = 21
GROUP = 24
NX, NY, NL, NH, NC = 4, 8, 2, 4, 2
N_CTX = NX * NY * NL
GRID = NX * NY
SENT = GRID * GROUP
ROWS = GRID * SLOTS
SHARE = ROWS // NH
LANES = 256
EXTRA = 8
PACK = 8 * SLOTS
PACK_SENT = 8 * GROUP
SLICE = D // (NH * NC)
CTX = ("x", "y", "l")
f32, bf16 = jnp.float32, jnp.bfloat16

epsilon = 1e-06


def swap(block, axis):
    return lax.ppermute(block, axis, [(0, 1), (1, 0)])


def exchange(blocks, axes):
    return lax.all_to_all(blocks, axes, split_axis=0, concat_axis=0, tiled=True)


def from_behind(block, distance):
    route = [(i, i + distance) for i in range(N_CTX - distance)]
    return lax.ppermute(block, CTX, route)


def attention(queries, key_rows, value_rows, strips):
    tokens = queries.shape[0]
    block = lax.axis_index(CTX)
    kv_first = lax.axis_index("h") // 2 * HD
    own = jnp.concatenate(
        [
            lax.dynamic_slice_in_dim(key_rows, kv_first, HD, 1),
            lax.dynamic_slice_in_dim(value_rows, kv_first, HD, 1),
        ],
        axis=1,
    )
    near = [from_behind(own, 2), from_behind(own, 1), own]
    sent, strips = lax.optimization_barrier((own, strips))
    pairs = [from_behind(sent, 3), *near]
    keys = jnp.concatenate([pair[:, :HD] for pair in pairs], axis=0)
    values = jnp.concatenate([pair[:, HD:] for pair in pairs], axis=0)
    q_view = queries.reshape(tokens, -1, HD)
    scores = jnp.einsum("tgd,sd->gts", q_view, keys, preferred_element_type=f32) / HD**0.5
    q_pos = block * tokens + jnp.arange(tokens)
    k_pos = (block - 3) * tokens + jnp.arange(4 * tokens)
    allowed = (k_pos[None, :] >= 0) & (k_pos[None, :] <= q_pos[:, None])
    scores = jnp.where(allowed, scores, -1e30)
    highest = jnp.max(scores, axis=2, keepdims=True)
    weights = jnp.where(allowed, jnp.exp(scores - highest), 0.0)
    denominators = jnp.sum(weights, axis=2, keepdims=True)
    mixed = (
        jnp.einsum("gts,sd->gtd", weights.astype(bf16), values, preferred_element_type=f32)
        / denominators
    )
    return jnp.transpose(mixed, (1, 0, 2)).reshape(tokens, -1).astype(bf16), strips


def slots_of(pred_ids, fix_pair, fix_expert, fix_count):
    tokens = pred_ids.shape[0]
    places = jnp.arange(tokens * TOPK, dtype=jnp.int32).reshape(tokens, TOPK)
    live = jnp.arange(FIX) < fix_count[0]
    hit = (places[:, :, None] == fix_pair[0][None, None, :]) & live[None, None, :]
    fixed = jnp.sum(jnp.where(hit, fix_expert[0][None, None, :], 0), axis=2)
    ids = jnp.where(jnp.any(hit, axis=2), fixed, pred_ids)
    named = ids[:, :, None] == jnp.arange(N_CTX)[None, None, :]
    counts = jnp.sum(named.astype(f32), axis=1)
    earlier = (
        jnp.arange(tokens)[:, None] > jnp.arange(tokens)[None, :]
    ).astype(bf16)
    before = jnp.dot(earlier, counts.astype(bf16), preferred_element_type=f32)
    rank = jnp.sum(jnp.where(named, before[:, None, :], 0.0), axis=2)
    twin = (ids[:, :, None] == ids[:, None, :]) & (
        jnp.arange(TOPK)[None, :, None] > jnp.arange(TOPK)[None, None, :]
    )
    rank = rank + jnp.sum(twin.astype(f32), axis=2)
    return ids.astype(f32), rank


def row_slots(table, side):
    ids, rank, gates = table[:TOPK], table[TOPK : 2 * TOPK], table[2 * TOPK :]
    column = jnp.floor(ids * 0.5)
    return jnp.where(ids - 2.0 * column == side, column * GROUP + rank, -1.0), gates


def spread(slots, values):
    row_ids = jnp.arange(SENT, dtype=f32)[:, None]
    total = jnp.zeros((SENT, slots.shape[1]), f32)
    for k in range(TOPK):
        total = total + jnp.where(slots[k][None, :] == row_ids, values[k][None, :], 0.0)
    return total.astype(bf16)


def packing():
    place = np.arange(PACK)
    return (place // SLOTS * GROUP + place % SLOTS)[:, None] == np.arange(PACK_SENT)[None, :]


def products_kernel(
    own_ref, other_ref, w_own_ref, w_other_ref, inv_own_ref, inv_other_ref, pick_ref, part_ref
):
    pick = pick_ref[...]
    ones = jnp.ones((8, SLICE), bf16)
    blank = jnp.zeros((LANES - SHARE, SLICE), bf16)
    row = lax.broadcasted_iota(jnp.int32, (EXTRA, FF), 0)

    def squares(rows, inverse_ref):
        weighted = (rows * rows * inverse_ref[...]).astype(bf16)
        return lax.dot_general(
            ones,
            jnp.concatenate([weighted, blank], axis=0),
            (((1,), (1,)), ((), ())),
            preferred_element_type=f32,
        )

    for h in range(NH):
        taken = slice(h * PACK_SENT, (h + 1) * PACK_SENT)
        own = jnp.dot(pick, own_ref[taken], preferred_element_type=f32)
        other = jnp.dot(pick, other_ref[taken], preferred_element_type=f32)
        part = jnp.dot(own.astype(bf16), w_own_ref[...], preferred_element_type=f32) + jnp.dot(
            other.astype(bf16), w_other_ref[...], preferred_element_type=f32
        )
        total = squares(own, inv_own_ref) + squares(other, inv_other_ref)
        total = jnp.concatenate([total, jnp.zeros((8, FF - LANES), f32)], axis=1)
        high = total.astype(bf16).astype(f32)
        tail = jnp.where(row == 0, high, jnp.where(row == 1, total - high, 0.0))
        part_ref[h] = jnp.concatenate([part, tail], axis=0).astype(bf16)


def products(own, other, w_own, w_other, inv_own, inv_other):
    return pl.pallas_call(
        products_kernel,
        out_shape=jax.ShapeDtypeStruct((NH, SHARE + EXTRA, FF), bf16),
        compiler_params=pltpu.CompilerParams(vmem_limit_bytes=48 * 1024 * 1024),
        cost_estimate=pl.CostEstimate(flops=100_000_000, bytes_accessed=500_000, transcendentals=0),
    )(own, other, w_own, w_other, inv_own, inv_other, jnp.asarray(packing(), bf16))


def results_kernel(own_ref, other_ref, down_own_ref, down_other_ref, place_ref, out_ref):
    place = place_ref[...]
    for i in range(NH // 2):
        rows = slice(2 * i * SHARE, 2 * (i + 1) * SHARE)
        part = jnp.dot(own_ref[rows], down_own_ref[...], preferred_element_type=f32) + jnp.dot(
            other_ref[rows], down_other_ref[...], preferred_element_type=f32
        )
        for j in range(2):
            rows = part[j * PACK : (j + 1) * PACK].astype(bf16)
            start = (2 * i + j) * PACK_SENT
            out_ref[start : start + PACK_SENT] = jnp.dot(
                place, rows, preferred_element_type=f32
            ).astype(bf16)


def expert_results(own, other, down_own, down_other):
    return pl.pallas_call(
        results_kernel,
        out_shape=jax.ShapeDtypeStruct((SENT, SLICE), bf16),
        compiler_params=pltpu.CompilerParams(vmem_limit_bytes=48 * 1024 * 1024),
        cost_estimate=pl.CostEstimate(flops=100_000_000, bytes_accessed=500_000, transcendentals=0),
    )(own, other, down_own, down_other, jnp.asarray(packing().T, bf16))


def activation_kernel(sums_ref, hidden_ref):
    sums = sums_ref[...].astype(f32)
    total = sums[SHARE : SHARE + 1, :LANES] + sums[SHARE + 1 : SHARE + 2, :LANES]
    scale = lax.rsqrt(total / D + epsilon)
    at = lax.broadcasted_iota(jnp.int32, (SHARE, LANES), 0)
    lane = lax.broadcasted_iota(jnp.int32, (SHARE, LANES), 1)
    scale = jnp.sum(jnp.where(at == lane, scale, 0.0), axis=1, keepdims=True)
    gate, up = sums[:SHARE, : FF // 2] * scale, sums[:SHARE, FF // 2 :] * scale
    hidden_ref[...] = (gate / (1.0 + jnp.exp(-gate)) * up).astype(bf16)


def activated(sums):
    return pl.pallas_call(
        activation_kernel,
        out_shape=jax.ShapeDtypeStruct((SHARE, FF // 2), bf16),
        compiler_params=pltpu.CompilerParams(vmem_limit_bytes=32 * 1024 * 1024),
        cost_estimate=pl.CostEstimate(flops=1_000_000, bytes_accessed=100_000, transcendentals=0),
    )(sums)


def body(
    queries,
    key_rows,
    value_rows,
    out_weight,
    residual,
    norm_gain,
    w_gate,
    w_up,
    w_down,
    pred_ids,
    route_gates,
    fix_pair,
    fix_expert,
    fix_count,
):
    core, side = lax.axis_index("c"), lax.axis_index("l")
    tokens = queries.shape[0]
    half = FF // 2

    other_strip = swap(out_weight, "l")
    strips = jnp.where(
        side == 0,
        jnp.concatenate([out_weight, other_strip], axis=0),
        jnp.concatenate([other_strip, out_weight], axis=0),
    )
    attended, strips = attention(queries, key_rows, value_rows, strips)
    quarter = lax.all_gather(strips, "y", axis=0, tiled=True)

    attended, pred_ids, fix_pair = lax.optimization_barrier((attended, pred_ids, fix_pair))
    ids, rank = slots_of(pred_ids, fix_pair, fix_expert, fix_count)
    table = jnp.concatenate([ids, rank, route_gates.astype(f32)], axis=1)
    slots, gates = row_slots(table.T, side.astype(f32))
    pick = spread(slots, jnp.ones_like(slots))

    heads = lax.all_gather(attended, "h", axis=0, tiled=True).reshape(NH, tokens, SLICE)
    other_slots, other_gates = row_slots(swap(table, "l").T, side.astype(f32))
    heads = exchange(heads, "x").reshape(NX * tokens, SLICE)
    heads, other_slots = lax.optimization_barrier((heads, other_slots))
    other_heads = swap(heads, "c")
    partial = jnp.dot(
        heads,
        lax.dynamic_slice_in_dim(quarter, core * SLICE, SLICE, 0),
        preferred_element_type=f32,
    ) + jnp.dot(
        other_heads,
        lax.dynamic_slice_in_dim(quarter, (1 - core) * SLICE, SLICE, 0),
        preferred_element_type=f32,
    )
    partial, w_gate, w_up, norm_gain = lax.optimization_barrier(
        (partial.astype(bf16), w_gate, w_up, norm_gain)
    )

    def columns(which):
        return jnp.concatenate(
            [
                lax.dynamic_slice_in_dim(w_gate[0], which * half, half, 1),
                lax.dynamic_slice_in_dim(w_up[0], which * half, half, 1),
            ],
            axis=1,
        )

    gate_up, other_gate_up = columns(core), swap(columns(1 - core), "c")
    down = lax.dynamic_slice_in_dim(w_down[0], core * half, half, 0)
    other_down = lax.dynamic_slice_in_dim(w_down[0], (1 - core) * half, half, 0)
    gain = norm_gain[None, :]
    inverse = 1.0 / (gain * gain)
    other_inverse = swap(inverse, "c")

    terms = exchange(partial.reshape(NX, tokens, SLICE), "x")
    other_pick = spread(other_slots, jnp.ones_like(other_slots))
    terms, other_pick = lax.optimization_barrier((terms, other_pick))
    stream = residual.astype(f32) + jnp.sum(terms.astype(f32), axis=0)

    scaled = (stream * gain).astype(bf16)
    beside = swap(scaled, "l")

    def through(rows):
        return exchange(rows.reshape(GRID, GROUP, SLICE), ("x", "y")).reshape(SENT, SLICE)

    def sent(pick, rows):
        return through(jnp.dot(pick, rows, preferred_element_type=f32).astype(bf16))

    def share_products(rows):
        return products(rows, swap(rows, "c"), gate_up, other_gate_up, inverse, other_inverse)

    def reduced(part):
        flat = part.reshape(NH * (SHARE + EXTRA), FF)
        return lax.psum_scatter(flat, "h", scatter_dimension=0, tiled=True)

    def gathered(sums):
        return lax.all_gather(activated(sums), "h", axis=0, tiled=True)

    def finished(hidden):
        return expert_results(hidden, swap(hidden, "c"), down, other_down)

    first = sent(other_pick, beside)
    first, pick, gate_up, other_gate_up, inverse, other_inverse = lax.optimization_barrier(
        (first, pick, gate_up, other_gate_up, inverse, other_inverse)
    )
    first = reduced(share_products(first))
    second = sent(pick, scaled)
    first, second = lax.optimization_barrier((first, second))
    second = reduced(share_products(second))
    first = through(finished(gathered(first)))
    hidden = gathered(second)
    combine = spread(slots, gates)
    first, hidden, combine = lax.optimization_barrier((first, hidden, combine))
    second = through(finished(hidden))
    other_mixed = jnp.einsum(
        "rt,rd->td", spread(other_slots, other_gates), first, preferred_element_type=f32
    )
    mixed = jnp.einsum("rt,rd->td", combine, second, preferred_element_type=f32)
    expert_out = mixed + swap(other_mixed.astype(bf16), "l").astype(f32)
    return stream.astype(bf16), expert_out.astype(bf16)


def solution(mesh):
    split = Mesh(np.asarray(mesh.devices).reshape(NX, NY, NL, NH, NC), ("x", "y", "l", "h", "c"))
    ctx, exp = CTX, ("h", "c")
    placed = (
        P(ctx, exp),
        P(ctx, None),
        P(ctx, None),
        P(ctx, exp),
        P(ctx, exp),
        P(exp),
        P(ctx, exp, None),
        P(ctx, exp, None),
        P(ctx, None, exp),
        P(ctx, None),
        P(ctx, None),
        P(ctx, None),
        P(ctx, None),
        P(ctx),
    )
    return jax.shard_map(
        body,
        mesh=split,
        in_specs=placed,
        out_specs=(P(ctx, exp), P(ctx, exp)),
        check_vma=False,
    )
```

```python
import jax
import jax.numpy as jnp
import numpy as np
from jax import lax
from jax.experimental import pallas as pl
from jax.experimental.pallas import tpu as pltpu
from jax.sharding import Mesh, PartitionSpec as P

D = 4096
HD = 128
TOPK = 8
QH = 32
KVH = 2
FF = 768
FIX = 32
TOK = 128
SLOTS = 21
GROUP = 24
NX, NY, NL, NH, NC = 4, 8, 2, 4, 2
N_CTX = NX * NY * NL
GRID = NX * NY
SENT = GRID * GROUP
ROWS = GRID * SLOTS
SHARE = ROWS // NH
LANES = 256
EXTRA = 8
PACK = 8 * SLOTS
PACK_SENT = 8 * GROUP
SLICE = D // (NH * NC)
CTX = ("x", "y", "l")
f32, bf16 = jnp.float32, jnp.bfloat16

epsilon = 1e-06


def swap(block, axis):
    return lax.ppermute(block, axis, [(0, 1), (1, 0)])


def exchange(blocks, axes):
    return lax.all_to_all(blocks, axes, split_axis=0, concat_axis=0, tiled=True)


def from_behind(block, distance):
    route = [(i, i + distance) for i in range(N_CTX - distance)]
    return lax.ppermute(block, CTX, route)


def attention(queries, key_rows, value_rows):
    tokens = queries.shape[0]
    block = lax.axis_index(CTX)
    kv_first = lax.axis_index("h") // 2 * HD
    own = jnp.concatenate(
        [
            lax.dynamic_slice_in_dim(key_rows, kv_first, HD, 1),
            lax.dynamic_slice_in_dim(value_rows, kv_first, HD, 1),
        ],
        axis=1,
    )
    pairs = [from_behind(own, 3), from_behind(own, 2), from_behind(own, 1), own]
    keys = jnp.concatenate([pair[:, :HD] for pair in pairs], axis=0)
    values = jnp.concatenate([pair[:, HD:] for pair in pairs], axis=0)
    q_view = queries.reshape(tokens, -1, HD)
    scores = jnp.einsum("tgd,sd->gts", q_view, keys, preferred_element_type=f32) / HD**0.5
    q_pos = block * tokens + jnp.arange(tokens)
    k_pos = (block - 3) * tokens + jnp.arange(4 * tokens)
    allowed = (k_pos[None, :] >= 0) & (k_pos[None, :] <= q_pos[:, None])
    scores = jnp.where(allowed, scores, -1e30)
    highest = jnp.max(scores, axis=2, keepdims=True)
    weights = jnp.where(allowed, jnp.exp(scores - highest), 0.0)
    denominators = jnp.sum(weights, axis=2, keepdims=True)
    mixed = (
        jnp.einsum("gts,sd->gtd", weights.astype(bf16), values, preferred_element_type=f32)
        / denominators
    )
    return jnp.transpose(mixed, (1, 0, 2)).reshape(tokens, -1).astype(bf16)


def slots_of(pred_ids, fix_pair, fix_expert, fix_count):
    tokens = pred_ids.shape[0]
    places = jnp.arange(tokens * TOPK, dtype=jnp.int32).reshape(tokens, TOPK)
    live = jnp.arange(FIX) < fix_count[0]
    hit = (places[:, :, None] == fix_pair[0][None, None, :]) & live[None, None, :]
    fixed = jnp.sum(jnp.where(hit, fix_expert[0][None, None, :], 0), axis=2)
    ids = jnp.where(jnp.any(hit, axis=2), fixed, pred_ids)
    named = ids[:, :, None] == jnp.arange(N_CTX)[None, None, :]
    counts = jnp.sum(named.astype(f32), axis=1)
    earlier = (
        jnp.arange(tokens)[:, None] > jnp.arange(tokens)[None, :]
    ).astype(bf16)
    before = jnp.dot(earlier, counts.astype(bf16), preferred_element_type=f32)
    rank = jnp.sum(jnp.where(named, before[:, None, :], 0.0), axis=2)
    twin = (ids[:, :, None] == ids[:, None, :]) & (
        jnp.arange(TOPK)[None, :, None] > jnp.arange(TOPK)[None, None, :]
    )
    rank = rank + jnp.sum(twin.astype(f32), axis=2)
    return ids.astype(f32), rank


def row_slots(table, side):
    ids, rank, gates = table[:TOPK], table[TOPK : 2 * TOPK], table[2 * TOPK :]
    column = jnp.floor(ids * 0.5)
    return jnp.where(ids - 2.0 * column == side, column * GROUP + rank, -1.0), gates


def spread(slots, values):
    row_ids = jnp.arange(SENT, dtype=f32)[:, None]
    total = jnp.zeros((SENT, slots.shape[1]), f32)
    for k in range(TOPK):
        total = total + jnp.where(slots[k][None, :] == row_ids, values[k][None, :], 0.0)
    return total.astype(bf16)


def packing():
    place = np.arange(PACK)
    return (place // SLOTS * GROUP + place % SLOTS)[:, None] == np.arange(PACK_SENT)[None, :]


def products_kernel(
    own_ref, other_ref, w_own_ref, w_other_ref, inv_own_ref, inv_other_ref, pick_ref, part_ref
):
    pick = pick_ref[...]
    ones = jnp.ones((8, SLICE), bf16)
    blank = jnp.zeros((LANES - SHARE, SLICE), bf16)
    row = lax.broadcasted_iota(jnp.int32, (EXTRA, FF), 0)

    def squares(rows, inverse_ref):
        weighted = (rows * rows * inverse_ref[...]).astype(bf16)
        return lax.dot_general(
            ones,
            jnp.concatenate([weighted, blank], axis=0),
            (((1,), (1,)), ((), ())),
            preferred_element_type=f32,
        )

    for h in range(NH):
        taken = slice(h * PACK_SENT, (h + 1) * PACK_SENT)
        own = jnp.dot(pick, own_ref[taken], preferred_element_type=f32)
        other = jnp.dot(pick, other_ref[taken], preferred_element_type=f32)
        part = jnp.dot(own.astype(bf16), w_own_ref[...], preferred_element_type=f32) + jnp.dot(
            other.astype(bf16), w_other_ref[...], preferred_element_type=f32
        )
        total = squares(own, inv_own_ref) + squares(other, inv_other_ref)
        total = jnp.concatenate([total, jnp.zeros((8, FF - LANES), f32)], axis=1)
        high = total.astype(bf16).astype(f32)
        tail = jnp.where(row == 0, high, jnp.where(row == 1, total - high, 0.0))
        part_ref[h] = jnp.concatenate([part, tail], axis=0).astype(bf16)


def products(own, other, w_own, w_other, inv_own, inv_other):
    return pl.pallas_call(
        products_kernel,
        out_shape=jax.ShapeDtypeStruct((NH, SHARE + EXTRA, FF), bf16),
        compiler_params=pltpu.CompilerParams(vmem_limit_bytes=48 * 1024 * 1024),
        cost_estimate=pl.CostEstimate(flops=100_000_000, bytes_accessed=500_000, transcendentals=0),
    )(own, other, w_own, w_other, inv_own, inv_other, jnp.asarray(packing(), bf16))


def results_kernel(own_ref, other_ref, down_own_ref, down_other_ref, place_ref, out_ref):
    place = place_ref[...]
    for i in range(NH // 2):
        rows = slice(2 * i * SHARE, 2 * (i + 1) * SHARE)
        part = jnp.dot(own_ref[rows], down_own_ref[...], preferred_element_type=f32) + jnp.dot(
            other_ref[rows], down_other_ref[...], preferred_element_type=f32
        )
        for j in range(2):
            rows = part[j * PACK : (j + 1) * PACK].astype(bf16)
            start = (2 * i + j) * PACK_SENT
            out_ref[start : start + PACK_SENT] = jnp.dot(
                place, rows, preferred_element_type=f32
            ).astype(bf16)


def expert_results(own, other, down_own, down_other):
    return pl.pallas_call(
        results_kernel,
        out_shape=jax.ShapeDtypeStruct((SENT, SLICE), bf16),
        compiler_params=pltpu.CompilerParams(vmem_limit_bytes=48 * 1024 * 1024),
        cost_estimate=pl.CostEstimate(flops=100_000_000, bytes_accessed=500_000, transcendentals=0),
    )(own, other, down_own, down_other, jnp.asarray(packing().T, bf16))


def activation_kernel(sums_ref, hidden_ref):
    sums = sums_ref[...].astype(f32)
    total = sums[SHARE : SHARE + 1, :LANES] + sums[SHARE + 1 : SHARE + 2, :LANES]
    scale = lax.rsqrt(total / D + epsilon)
    at = lax.broadcasted_iota(jnp.int32, (SHARE, LANES), 0)
    lane = lax.broadcasted_iota(jnp.int32, (SHARE, LANES), 1)
    scale = jnp.sum(jnp.where(at == lane, scale, 0.0), axis=1, keepdims=True)
    gate, up = sums[:SHARE, : FF // 2] * scale, sums[:SHARE, FF // 2 :] * scale
    hidden_ref[...] = (gate / (1.0 + jnp.exp(-gate)) * up).astype(bf16)


def activated(sums):
    return pl.pallas_call(
        activation_kernel,
        out_shape=jax.ShapeDtypeStruct((SHARE, FF // 2), bf16),
        compiler_params=pltpu.CompilerParams(vmem_limit_bytes=32 * 1024 * 1024),
        cost_estimate=pl.CostEstimate(flops=1_000_000, bytes_accessed=100_000, transcendentals=0),
    )(sums)


def body(
    queries,
    key_rows,
    value_rows,
    out_weight,
    residual,
    norm_gain,
    w_gate,
    w_up,
    w_down,
    pred_ids,
    route_gates,
    fix_pair,
    fix_expert,
    fix_count,
):
    core, side = lax.axis_index("c"), lax.axis_index("l")
    tokens = queries.shape[0]
    half = FF // 2

    attended = attention(queries, key_rows, value_rows)

    other_strip = swap(out_weight, "l")
    attended, other_strip = lax.optimization_barrier((attended, other_strip))
    strips = jnp.where(
        side == 0,
        jnp.concatenate([out_weight, other_strip], axis=0),
        jnp.concatenate([other_strip, out_weight], axis=0),
    )
    strips, attended = lax.optimization_barrier((strips, attended))
    quarter = lax.all_gather(strips, "y", axis=0, tiled=True)

    attended, pred_ids, fix_pair = lax.optimization_barrier((attended, pred_ids, fix_pair))
    ids, rank = slots_of(pred_ids, fix_pair, fix_expert, fix_count)
    table = jnp.concatenate([ids, rank, route_gates.astype(f32)], axis=1)
    slots, gates = row_slots(table.T, side.astype(f32))
    pick = spread(slots, jnp.ones_like(slots))

    heads = exchange(jnp.broadcast_to(attended[None], (NH, *attended.shape)), "h")
    other_slots, other_gates = row_slots(swap(table, "l").T, side.astype(f32))
    heads = exchange(heads, "x").reshape(NX * tokens, SLICE)
    heads, other_slots = lax.optimization_barrier((heads, other_slots))
    other_heads = swap(heads, "c")
    partial = jnp.dot(
        heads,
        lax.dynamic_slice_in_dim(quarter, core * SLICE, SLICE, 0),
        preferred_element_type=f32,
    ) + jnp.dot(
        other_heads,
        lax.dynamic_slice_in_dim(quarter, (1 - core) * SLICE, SLICE, 0),
        preferred_element_type=f32,
    )
    partial, w_gate, w_up, norm_gain = lax.optimization_barrier(
        (partial.astype(bf16), w_gate, w_up, norm_gain)
    )

    def columns(which):
        return jnp.concatenate(
            [
                lax.dynamic_slice_in_dim(w_gate[0], which * half, half, 1),
                lax.dynamic_slice_in_dim(w_up[0], which * half, half, 1),
            ],
            axis=1,
        )

    gate_up, other_gate_up = columns(core), swap(columns(1 - core), "c")
    down = lax.dynamic_slice_in_dim(w_down[0], core * half, half, 0)
    other_down = lax.dynamic_slice_in_dim(w_down[0], (1 - core) * half, half, 0)
    gain = norm_gain[None, :]
    inverse = 1.0 / (gain * gain)
    other_inverse = swap(inverse, "c")

    terms = exchange(partial.reshape(NX, tokens, SLICE), "x")
    other_pick = spread(other_slots, jnp.ones_like(other_slots))
    terms, other_pick = lax.optimization_barrier((terms, other_pick))
    stream = residual.astype(f32) + jnp.sum(terms.astype(f32), axis=0)

    scaled = (stream * gain).astype(bf16)
    beside = swap(scaled, "l")

    def through(rows):
        return exchange(rows.reshape(GRID, GROUP, SLICE), ("x", "y")).reshape(SENT, SLICE)

    def sent(pick, rows):
        return through(jnp.dot(pick, rows, preferred_element_type=f32).astype(bf16))

    def share_products(rows):
        return products(rows, swap(rows, "c"), gate_up, other_gate_up, inverse, other_inverse)

    def reduced(part):
        flat = part.reshape(NH * (SHARE + EXTRA), FF)
        return lax.psum_scatter(flat, "h", scatter_dimension=0, tiled=True)

    def gathered(sums):
        return lax.all_gather(activated(sums), "h", axis=0, tiled=True)

    def finished(hidden):
        return expert_results(hidden, swap(hidden, "c"), down, other_down)

    first = sent(other_pick, beside)
    first, pick, gate_up, other_gate_up, inverse, other_inverse = lax.optimization_barrier(
        (first, pick, gate_up, other_gate_up, inverse, other_inverse)
    )
    first = reduced(share_products(first))
    second = sent(pick, scaled)
    first, second = lax.optimization_barrier((first, second))
    second = reduced(share_products(second))
    first = through(finished(gathered(first)))
    hidden = gathered(second)
    combine = spread(slots, gates)
    first, hidden, combine = lax.optimization_barrier((first, hidden, combine))
    second = through(finished(hidden))
    other_mixed = jnp.einsum(
        "rt,rd->td", spread(other_slots, other_gates), first, preferred_element_type=f32
    )
    mixed = jnp.einsum("rt,rd->td", combine, second, preferred_element_type=f32)
    expert_out = mixed + swap(other_mixed.astype(bf16), "l").astype(f32)
    return stream.astype(bf16), expert_out.astype(bf16)


def solution(mesh):
    split = Mesh(np.asarray(mesh.devices).reshape(NX, NY, NL, NH, NC), ("x", "y", "l", "h", "c"))
    ctx, exp = CTX, ("h", "c")
    placed = (
        P(ctx, exp),
        P(ctx, None),
        P(ctx, None),
        P(ctx, exp),
        P(ctx, exp),
        P(exp),
        P(ctx, exp, None),
        P(ctx, exp, None),
        P(ctx, None, exp),
        P(ctx, None),
        P(ctx, None),
        P(ctx, None),
        P(ctx, None),
        P(ctx),
    )
    return jax.shard_map(
        body,
        mesh=split,
        in_specs=placed,
        out_specs=(P(ctx, exp), P(ctx, exp)),
        check_vma=False,
    )
```
